512 devices in a mesh: dp: 64 (over x, z, core), tensor: 8 (over y).
Axes of the slice: x: 4, y: 8, z: 8, core: 2. Of those that a mesh axis runs over, the one named last changes fastest.
Arguments:
- tokens: bfloat16 [24576, 4096], P('dp', 'tensor'), may hold values from -6 to 6
- w_gate: bfloat16 [640, 4096], P('tensor'), may hold values from -0.09375 to 0.09375
- w_up: bfloat16 [640, 4096], P('tensor'), may hold values from -0.09375 to 0.09375
- d_hidden: bfloat16 [24576, 640], P('dp', 'tensor'), may hold values from -6 to 6
- error_fb: bfloat16 [64, 2, 640, 4096], P('dp', None, 'tensor'), may hold values from -3 to 3
- q_prev: float32 [2, 640, 64], P(None, 'tensor'), may hold values from -6 to 6
Outputs:
- d_tokens: bfloat16 [24576, 4096], P('dp', 'tensor')
- new_error: bfloat16 [64, 2, 640, 4096], P('dp', None, 'tensor')
- q_next: float32 [2, 640, 64], P(None, 'tensor')
The draws below stay inside these ranges and needn't reach their ends.
All inputs are finite; a program needn't handle non-finite values.
Results may differ from the reference program's by a relative error of at most 0.017.
Values may be sent and summed in bfloat16 or wider, within the bound.
No kernel may reach another device: no remote copies, remote signals or barrier semaphores. Data moves between devices by JAX's collectives and lax.ppermute only.
A program may use at most 64 MiB of HBM per device.

```python
import math
import jax
import jax.numpy as jnp
from jax import lax

D = 4096
BUCKET = 80
RANK = 64
TOK_DEV = 384
TOKENS = 24576
HIDDEN_ROWS = 640
N_DP = 64
N_TENSOR = 8


def block_scale(stream_key, dims, shards, least, largest):
    def one(dim, shards_of):
        steps = jax.random.uniform(jax.random.fold_in(jax.random.fold_in(stream_key, 6), dim), (shards_of,), jnp.float32, least / len(shards), largest / len(shards))
        return jnp.repeat(jnp.exp(steps), dims[dim] // shards_of).reshape((-1,) + (1,) * (len(dims) - dim - 1))

    gain = one(*shards[0])
    for cut in shards[1:]:
        gain = gain * one(*cut)
    return gain


def normal_values(rng, shape, deviation, bound, cuts=(), held_as=jnp.bfloat16):
    values = jax.random.normal(rng, shape, jnp.float32) * deviation
    if len(cuts) > 0:
        values = block_scale(rng, shape, cuts, -0.22, 0.18) * values
    return jnp.clip(values, min=-bound, max=bound).astype(held_as)


def setup_inputs(seed: int = 0) -> dict:
    keys = jax.random.split(jax.random.key(seed), 7)
    return {
        "tokens": normal_values(keys[0], (TOKENS, D), 1.0, 6.0, ((0, 64), (1, 8))),
        "w_gate": normal_values(keys[1], (HIDDEN_ROWS, D), D ** -0.5, 0.09375, ((0, 8),)),
        "w_up": normal_values(keys[2], (HIDDEN_ROWS, D), D ** -0.5, 0.09375, ((0, 8),)),
        "d_hidden": normal_values(keys[3], (TOKENS, HIDDEN_ROWS), 1.0, 6.0, ((0, 64), (1, 8))),
        "error_fb": normal_values(keys[4], (N_DP, 2, HIDDEN_ROWS, D), 0.5, 3.0, ((0, 64), (2, 8))),
        "q_prev": normal_values(keys[5], (2, HIDDEN_ROWS, RANK), 1.0, 6.0, ((1, 8),), jnp.float32),
    }


HIGH_PRECISION = lax.Precision.HIGHEST

def shard_terms(tok_rows, w_gate_rows, w_up_rows, cot_rows, feedback, q_matrix):
    contract_last = (((1,), (1,)), ((), ()))
    contract_first = (((0,), (0,)), ((), ()))
    gate_pre = lax.dot_general(tok_rows.astype(jnp.float32), w_gate_rows.astype(jnp.float32), contract_last, preferred_element_type=jnp.float32)
    up_pre = lax.dot_general(tok_rows.astype(jnp.float32), w_up_rows.astype(jnp.float32), contract_last, preferred_element_type=jnp.float32)
    squash = jax.nn.sigmoid(gate_pre)
    upstream = cot_rows.astype(jnp.float32)
    d_gate = (upstream * up_pre * squash * (1.0 + gate_pre * (1.0 - squash))).astype(jnp.bfloat16)
    d_up = (upstream * gate_pre * squash).astype(jnp.bfloat16)
    act_terms = jnp.dot(d_gate.astype(jnp.float32), w_gate_rows.astype(jnp.float32), preferred_element_type=jnp.float32) + jnp.dot(d_up.astype(jnp.float32), w_up_rows.astype(jnp.float32), preferred_element_type=jnp.float32)
    grads = jnp.concatenate([lax.dot_general(d_gate.astype(jnp.float32), tok_rows.astype(jnp.float32), contract_first, preferred_element_type=jnp.float32), lax.dot_general(d_up.astype(jnp.float32), tok_rows.astype(jnp.float32), contract_first, preferred_element_type=jnp.float32)], 0)
    merged = grads * (1.0 / math.sqrt(TOK_DEV)) + feedback.reshape(grads.shape).astype(jnp.float32)
    p_local = lax.dot_general(q_matrix.astype(jnp.float32), merged.astype(jnp.float32), contract_first, precision=HIGH_PRECISION, preferred_element_type=jnp.float32)
    return (act_terms.astype(jnp.bfloat16), merged, p_local)

def orthonormal(p_matrix):
    gram_matrix = jnp.dot(p_matrix, p_matrix.T, precision=HIGH_PRECISION)
    lower_factor = jnp.linalg.cholesky(gram_matrix)
    return jax.scipy.linalg.solve_triangular(lower_factor, p_matrix, lower=True)

def reference(tokens, w_gate, w_up, d_hidden, error_fb, q_prev):
    tok_blocks = tokens.reshape(N_DP, TOK_DEV, D)
    cot_blocks = jnp.moveaxis(d_hidden.reshape(N_DP, TOK_DEV, N_TENSOR, BUCKET), 2, 0)
    gate_blocks = w_gate.reshape(N_TENSOR, BUCKET, D)
    up_blocks = w_up.reshape(N_TENSOR, BUCKET, D)
    fb_blocks = jnp.moveaxis(error_fb.reshape(N_DP, 2, N_TENSOR, BUCKET, D), 2, 0)
    q_blocks = jnp.moveaxis(q_prev.reshape(2, N_TENSOR, BUCKET, RANK), 1, 0)

    def one_group(summed, pieces):
        w_gate_rows, w_up_rows, cot_rows, fb_rows, q_rows = pieces
        q_matrix = q_rows.reshape(2 * BUCKET, RANK)
        act_terms, merged, p_local = jax.vmap(shard_terms, in_axes=(0, None, None, 0, 0, None))(tok_blocks, w_gate_rows, w_up_rows, cot_rows, fb_rows, q_matrix)
        p_mean = lax.optimization_barrier(jnp.sum(p_local, axis=0)) / N_DP
        p_orth = orthonormal(p_mean)
        q_local = jnp.einsum('nhd,rd->nhr', merged, p_orth, precision=HIGH_PRECISION)
        q_group = lax.optimization_barrier(jnp.sum(q_local, axis=0)) / N_DP
        approximation = jnp.dot(q_group, p_orth, precision=HIGH_PRECISION)
        fresh = (merged - approximation[None]).astype(jnp.bfloat16)
        return (summed + act_terms.astype(jnp.float32), (fresh, q_group))
    start = jnp.zeros((N_DP, TOK_DEV, D), jnp.float32)
    summed, (fresh_all, q_all) = lax.scan(one_group, start, (gate_blocks, up_blocks, cot_blocks, fb_blocks, q_blocks))
    d_tokens = summed.astype(jnp.bfloat16).reshape(TOKENS, D)
    new_error = jnp.transpose(fresh_all.reshape(N_TENSOR, N_DP, 2, BUCKET, D), (1, 2, 0, 3, 4)).reshape(N_DP, 2, N_TENSOR * BUCKET, D)
    q_next = jnp.transpose(q_all.reshape(N_TENSOR, 2, BUCKET, RANK), (1, 0, 2, 3)).reshape(2, N_TENSOR * BUCKET, RANK)
    return (d_tokens, new_error, q_next)
```

```python
import math

import jax
import jax.numpy as jnp
from jax import lax
from jax.sharding import Mesh, PartitionSpec as P

HIGH_PRECISION = lax.Precision.HIGHEST
LANES = 128


def mean_over_workers(local, workers):
    chips = ("x", "z")
    n_chips = lax.axis_size(chips)
    rows, width = local.shape[0] // 2, local.shape[1]
    piece = width // n_chips
    core = lax.axis_index("core")
    halves = local.reshape(2, rows, width)
    mine = lax.dynamic_index_in_dim(halves, core, 0, keepdims=False)
    other = lax.dynamic_index_in_dim(halves, 1 - core, 0, keepdims=False)
    got = lax.ppermute(other.astype(jnp.bfloat16), "core", [(0, 1), (1, 0)])
    pair = (mine.astype(jnp.float32) + got.astype(jnp.float32)).astype(jnp.bfloat16)
    pieces = pair.reshape(rows, n_chips, piece).transpose(1, 0, 2)
    pieces = lax.all_to_all(pieces, chips, 0, 0, tiled=True)
    total = jnp.sum(pieces.astype(jnp.float32), 0) * (1.0 / workers)
    copies = jnp.broadcast_to(total.astype(jnp.bfloat16)[None], (n_chips, rows, piece))
    gathered = lax.all_to_all(copies, chips, 0, 0, tiled=True)
    half = gathered.transpose(1, 0, 2).reshape(rows, width)
    return lax.all_gather(half, "core", axis=0, tiled=True).astype(jnp.float32)


def on_device(tokens, w_gate, w_up, d_hidden, error_fb, q_prev):
    contract_last = (((1,), (1,)), ((), ()))
    contract_first = (((0,), (0,)), ((), ()))
    whole = lax.all_gather(tokens, "tensor", axis=1, tiled=True)
    gate_pre = lax.dot_general(whole, w_gate, contract_last, preferred_element_type=jnp.float32)
    up_pre = lax.dot_general(whole, w_up, contract_last, preferred_element_type=jnp.float32)
    squash = jax.nn.sigmoid(gate_pre)
    upstream = d_hidden.astype(jnp.float32)
    d_gate = (upstream * up_pre * squash * (1.0 + gate_pre * (1.0 - squash))).astype(jnp.bfloat16)
    d_up = (upstream * gate_pre * squash).astype(jnp.bfloat16)
    act_terms = jnp.dot(d_gate, w_gate, preferred_element_type=jnp.float32) + jnp.dot(
        d_up, w_up, preferred_element_type=jnp.float32
    )
    d_tokens = lax.psum_scatter(act_terms.astype(jnp.bfloat16), "tensor", scatter_dimension=1, tiled=True)
    grads = jnp.concatenate(
        [
            lax.dot_general(d_gate, whole, contract_first, preferred_element_type=jnp.float32),
            lax.dot_general(d_up, whole, contract_first, preferred_element_type=jnp.float32),
        ],
        0,
    )
    grad_scale = 1.0 / math.sqrt(whole.shape[0])
    merged = grads * grad_scale + error_fb.reshape(grads.shape).astype(jnp.float32)
    q_matrix = q_prev.reshape(grads.shape[0], q_prev.shape[2])
    mean = mean_over_workers(merged, lax.axis_size(("x", "z", "core")))
    p_mean = lax.dot_general(
        q_matrix, mean, contract_first, precision=HIGH_PRECISION, preferred_element_type=jnp.float32
    )
    gram_matrix = jnp.dot(p_mean, p_mean.T, precision=HIGH_PRECISION)
    lower_factor = jnp.linalg.cholesky(gram_matrix)
    p_orth = jax.scipy.linalg.solve_triangular(lower_factor, p_mean, lower=True)
    q_group = lax.dot_general(
        mean, p_orth, contract_last, precision=HIGH_PRECISION, preferred_element_type=jnp.float32
    )
    approximation = jnp.dot(q_group, p_orth, precision=HIGH_PRECISION)
    new_error = (merged - approximation).astype(jnp.bfloat16).reshape(error_fb.shape)
    return (d_tokens, new_error, q_group.reshape(q_prev.shape))


def solution(mesh):
    chips_apart = Mesh(mesh.devices.reshape(4, 8, 2, 8), ("x", "z", "core", "tensor"))
    dp = ("x", "z", "core")
    return jax.shard_map(
        on_device,
        mesh=chips_apart,
        in_specs=(
            P(dp, "tensor"),
            P("tensor", None),
            P("tensor", None),
            P(dp, "tensor"),
            P(dp, None, "tensor", None),
            P(None, "tensor", None),
        ),
        out_specs=(P(dp, "tensor"), P(dp, None, "tensor", None), P(None, "tensor", None)),
        check_vma=False,
    )
```

```python
import functools
import math

import jax
import jax.numpy as jnp
from jax import lax
from jax.experimental import pallas as pl
from jax.experimental.pallas import tpu as pltpu
from jax.sharding import Mesh, PartitionSpec as P

HIGH_PRECISION = lax.Precision.HIGHEST
CHIPS = ("x", "z")
SWAP = ((0, 1), (1, 0))
VMEM_BYTES = 50 * 1024 * 1024


def three_parts(value):
    high = value.astype(jnp.bfloat16)
    rest = value - high.astype(jnp.float32)
    middle = rest.astype(jnp.bfloat16)
    low = (rest - middle.astype(jnp.float32)).astype(jnp.bfloat16)
    return high, middle, low


def inverse_cholesky(gram):
    n = gram.shape[0]
    row_ids = lax.broadcasted_iota(jnp.int32, (n, n), 0)
    col_ids = lax.broadcasted_iota(jnp.int32, (n, n), 1)
    eye = jnp.where(row_ids == col_ids, 1.0, 0.0)
    work = jnp.concatenate([gram, eye], 1)
    blocks = [work[8 * k : 8 * k + 8] for k in range(n // 8)]
    below = lax.broadcasted_iota(jnp.int32, (8, 2 * n), 0)
    for j in range(n - 1):
        k, i = divmod(j, 8)
        row = blocks[k][i : i + 1]
        scaled = row * (1.0 / row[:, j : j + 1])
        for b in range(k, n // 8):
            factor = jnp.broadcast_to(blocks[b][:, j : j + 1], (8, 2 * n))
            if b == k:
                factor = jnp.where(below > i, factor, 0.0)
            blocks[b] = blocks[b] - factor * scaled
    work = jnp.concatenate(blocks, 0)
    pivots = jnp.sum(jnp.where(row_ids == col_ids, work[:, :n], 0.0), 1, keepdims=True)
    return work[:, n:] * lax.rsqrt(pivots)


def finish_kernel(core_ref, own_ref, other_ref, q_ref, merged_ref, new_ref, q_next_ref, stack_ref):
    chunks, rows, lanes = own_ref.shape
    units, rank = 2 * rows, q_ref.shape[1]
    first = core_ref[0] == 0
    for j in range(chunks):
        at = slice(j * lanes, (j + 1) * lanes)
        stack_ref[0:rows, at] = jnp.where(first, own_ref[j], other_ref[j])
        stack_ref[rows:units, at] = jnp.where(first, other_ref[j], own_ref[j])
    q_gate = jnp.concatenate(three_parts(q_ref[0]), 0)
    q_up = jnp.concatenate(three_parts(q_ref[1]), 0)
    width = chunks * lanes
    step = 1024
    for f in range(0, width, step):
        p_parts = jnp.dot(q_gate, stack_ref[0:rows, f : f + step], preferred_element_type=jnp.float32)
        p_parts += jnp.dot(q_up, stack_ref[rows:units, f : f + step], preferred_element_type=jnp.float32)
        p_mean = p_parts[0:rank] + p_parts[rank : 2 * rank] + p_parts[2 * rank :]
        for k, part in enumerate(three_parts(p_mean)):
            stack_ref[units + k * rank : units + (k + 1) * rank, f : f + step] = part
    products = lax.dot_general(
        stack_ref[...], stack_ref[units:, :], (((1,), (1,)), ((), ())), preferred_element_type=jnp.float32
    )
    products = products[:, 0:rank] + products[:, rank : 2 * rank] + products[:, 2 * rank :]
    gram = products[units : units + rank] + products[units + rank : units + 2 * rank] + products[units + 2 * rank :]
    inverse = inverse_cholesky(gram)
    for k in range(2):
        q_next_ref[k] = lax.dot_general(
            inverse, products[k * rows : (k + 1) * rows], (((1,), (1,)), ((), ())),
            precision=HIGH_PRECISION, preferred_element_type=jnp.float32,
        )
    gram_inverse = jnp.dot(inverse.T, inverse, precision=HIGH_PRECISION, preferred_element_type=jnp.float32)
    weights = jnp.dot(
        products[0:units], gram_inverse, precision=HIGH_PRECISION, preferred_element_type=jnp.float32
    )
    high, middle, _ = three_parts(weights)
    factors = jnp.concatenate([high, high, middle], 1)
    for f in range(0, width, step):
        p_high = stack_ref[units : units + rank, f : f + step]
        p_middle = stack_ref[units + rank : units + 2 * rank, f : f + step]
        basis = jnp.concatenate([p_high, p_middle, p_high], 0)
        approximation = jnp.dot(factors, basis, preferred_element_type=jnp.float32)
        fresh = (merged_ref[:, f : f + step] - approximation).astype(jnp.bfloat16)
        new_ref[0, :, f : f + step] = fresh[0:rows]
        new_ref[1, :, f : f + step] = fresh[rows:]


def finish(core, own, other, q_prev, merged):
    rows = own.shape[1]
    width = own.shape[0] * own.shape[2]
    rank = q_prev.shape[2]
    vmem = pl.BlockSpec(memory_space=pltpu.VMEM)
    return pl.pallas_call(
        finish_kernel,
        out_shape=(
            jax.ShapeDtypeStruct((2, rows, width), jnp.bfloat16),
            jax.ShapeDtypeStruct((2, rank, rows), jnp.float32),
        ),
        in_specs=[pl.BlockSpec(memory_space=pltpu.SMEM), vmem, vmem, vmem, vmem],
        out_specs=(vmem, vmem),
        scratch_shapes=[pltpu.VMEM((2 * rows + 3 * rank, width), jnp.bfloat16)],
        compiler_params=pltpu.CompilerParams(vmem_limit_bytes=VMEM_BYTES),
        name="finish",
    )(core.reshape(1), own, other, q_prev.transpose(0, 2, 1), merged)


def gradient_kernel(core_ref, tokens_hbm, gate_ref, up_ref, cot_ref, error_ref, d_ref, send_ref, keep_ref, merged_ref, tokens_ref, sems, *, scale):
    parts = sems.shape[0]
    rows, width = gate_ref.shape
    step = width // parts
    chunks, _, lanes = send_ref.shape

    def load(k):
        at = pl.ds(k * step, step)
        return pltpu.make_async_copy(tokens_hbm.at[:, at], tokens_ref.at[:, at], sems.at[k])

    for k in range(parts):
        load(k).start()
    pre = jnp.zeros((2 * rows, tokens_ref.shape[0]), jnp.float32)
    for k in range(parts):
        load(k).wait()
        at = slice(k * step, (k + 1) * step)
        weights = jnp.concatenate([gate_ref[:, at], up_ref[:, at]], 0)
        pre += lax.dot_general(
            weights, tokens_ref[:, at], (((1,), (1,)), ((), ())), preferred_element_type=jnp.float32
        )
    gate_pre, up_pre = pre[0:rows], pre[rows:]
    squash = jax.nn.sigmoid(gate_pre)
    upstream = cot_ref[...].astype(jnp.float32)
    d_gate = (upstream * up_pre * squash * (1.0 + gate_pre * (1.0 - squash))).astype(jnp.bfloat16)
    d_up = (upstream * gate_pre * squash).astype(jnp.bfloat16)
    d_both = jnp.concatenate([d_gate, d_up], 0)
    d_ref[...] = d_both
    first = core_ref[0] == 0
    step = 512
    for f in range(0, width, step):
        at = slice(f, f + step)
        grads = jnp.dot(d_both, tokens_ref[:, at], preferred_element_type=jnp.float32) * scale
        gate_half = grads[0:rows] + error_ref[0, :, at].astype(jnp.float32)
        up_half = grads[rows:] + error_ref[1, :, at].astype(jnp.float32)
        merged_ref[0:rows, at] = gate_half
        merged_ref[rows:, at] = up_half
        keep = jnp.where(first, gate_half, up_half)
        send = jnp.where(first, up_half, gate_half).astype(jnp.bfloat16)
        for i in range(step // lanes):
            part = slice(i * lanes, (i + 1) * lanes)
            keep_ref[f // lanes + i] = keep[:, part]
            send_ref[f // lanes + i] = send[:, part]


def gradients(core, whole, w_gate, w_up, cot, error_fb, n_chips):
    count, width = whole.shape
    rows = w_gate.shape[0]
    lanes = width // n_chips
    vmem = pl.BlockSpec(memory_space=pltpu.VMEM)
    return pl.pallas_call(
        functools.partial(gradient_kernel, scale=1.0 / math.sqrt(count)),
        out_shape=(
            jax.ShapeDtypeStruct((2 * rows, count), jnp.bfloat16),
            jax.ShapeDtypeStruct((n_chips, rows, lanes), jnp.bfloat16),
            jax.ShapeDtypeStruct((n_chips, rows, lanes), jnp.float32),
            jax.ShapeDtypeStruct((2 * rows, width), jnp.float32),
        ),
        in_specs=[pl.BlockSpec(memory_space=pltpu.SMEM), pl.BlockSpec(memory_space=pl.ANY)] + [vmem] * 4,
        out_specs=(vmem,) * 4,
        scratch_shapes=[pltpu.VMEM((count, width), jnp.bfloat16), pltpu.SemaphoreType.DMA((8,))],
        compiler_params=pltpu.CompilerParams(vmem_limit_bytes=VMEM_BYTES),
        name="gradients",
    )(core.reshape(1), whole, w_gate, w_up, cot.T, error_fb.reshape(2, rows, width))


def act_kernel(d_ref, gate_ref, up_ref, act_ref):
    d_both = d_ref[...].T
    step = 1024
    for f in range(0, act_ref.shape[1], step):
        at = slice(f, f + step)
        weights = jnp.concatenate([gate_ref[:, at], up_ref[:, at]], 0)
        act_ref[:, at] = jnp.dot(d_both, weights, preferred_element_type=jnp.float32).astype(jnp.bfloat16)


def act_terms(d_both, w_gate, w_up):
    vmem = pl.BlockSpec(memory_space=pltpu.VMEM)
    return pl.pallas_call(
        act_kernel,
        out_shape=jax.ShapeDtypeStruct((d_both.shape[1], w_gate.shape[1]), jnp.bfloat16),
        in_specs=[vmem] * 3,
        out_specs=vmem,
        compiler_params=pltpu.CompilerParams(vmem_limit_bytes=VMEM_BYTES),
        name="act_terms",
    )(d_both, w_gate, w_up)


def mean_kernel(pieces_ref, copies_ref, *, scale):
    total = pieces_ref[0].astype(jnp.float32)
    for k in range(1, pieces_ref.shape[0]):
        total += pieces_ref[k].astype(jnp.float32)
    mean = (total * scale).astype(jnp.bfloat16)
    for k in range(copies_ref.shape[0]):
        copies_ref[k] = mean


def mean_copies(pieces, workers):
    vmem = pl.BlockSpec(memory_space=pltpu.VMEM)
    return pl.pallas_call(
        functools.partial(mean_kernel, scale=1.0 / workers),
        out_shape=jax.ShapeDtypeStruct(pieces.shape, jnp.bfloat16),
        in_specs=[vmem],
        out_specs=vmem,
        compiler_params=pltpu.CompilerParams(vmem_limit_bytes=VMEM_BYTES),
        name="mean_copies",
    )(pieces)


def on_device(tokens, w_gate, w_up, d_hidden, error_fb, q_prev):
    core = lax.axis_index("core")
    n_chips = lax.axis_size(CHIPS)
    whole = lax.all_gather(tokens, "tensor", axis=1, tiled=True)
    d_both, send, keep, merged = gradients(core, whole, w_gate, w_up, d_hidden, error_fb, n_chips)
    act = act_terms(d_both, w_gate, w_up)
    got = lax.ppermute(send, "core", SWAP)
    pieces = (keep + got.astype(jnp.float32)).astype(jnp.bfloat16)
    pieces, act = lax.optimization_barrier((pieces, act))
    d_tokens = lax.psum_scatter(act, "tensor", scatter_dimension=1, tiled=True)
    pieces = lax.all_to_all(pieces, CHIPS, 0, 0, tiled=True)
    copies = mean_copies(pieces, n_chips * lax.axis_size("core"))
    own_half = lax.all_to_all(copies, CHIPS, 0, 0, tiled=True)
    other_half = lax.ppermute(own_half, "core", SWAP)
    new_error, q_next = finish(core, own_half, other_half, q_prev, merged)
    return (d_tokens, new_error.reshape(error_fb.shape), q_next.transpose(0, 2, 1))


def solution(mesh):
    chips_apart = Mesh(mesh.devices.reshape(4, 8, 2, 8), ("x", "z", "core", "tensor"))
    dp = ("x", "z", "core")
    return jax.shard_map(
        on_device,
        mesh=chips_apart,
        in_specs=(
            P(dp, "tensor"),
            P("tensor", None),
            P("tensor", None),
            P(dp, "tensor"),
            P(dp, None, "tensor", None),
            P(None, "tensor", None),
        ),
        out_specs=(P(dp, "tensor"), P(dp, None, "tensor", None), P(None, "tensor", None)),
        check_vma=False,
    )
```

```python
import functools
import math

import jax
import jax.numpy as jnp
from jax import lax
from jax.experimental import pallas as pl
from jax.experimental.pallas import tpu as pltpu
from jax.sharding import Mesh, PartitionSpec as P

HIGH_PRECISION = lax.Precision.HIGHEST
CHIPS = ("x", "z")
SWAP = ((0, 1), (1, 0))
VMEM_BYTES = 24 * 1024 * 1024


def three_parts(value):
    high = value.astype(jnp.bfloat16)
    rest = value - high.astype(jnp.float32)
    middle = rest.astype(jnp.bfloat16)
    low = (rest - middle.astype(jnp.float32)).astype(jnp.bfloat16)
    return high, middle, low


def inverse_cholesky(gram):
    n = gram.shape[0]
    row_ids = lax.broadcasted_iota(jnp.int32, (n, n), 0)
    col_ids = lax.broadcasted_iota(jnp.int32, (n, n), 1)
    eye = jnp.where(row_ids == col_ids, 1.0, 0.0)
    work = jnp.concatenate([gram, eye], 1)
    blocks = [work[8 * k : 8 * k + 8] for k in range(n // 8)]
    below = lax.broadcasted_iota(jnp.int32, (8, 2 * n), 0)
    for j in range(n - 1):
        k, i = divmod(j, 8)
        row = blocks[k][i : i + 1]
        scaled = row * (1.0 / row[:, j : j + 1])
        for b in range(k, n // 8):
            factor = jnp.broadcast_to(blocks[b][:, j : j + 1], (8, 2 * n))
            if b == k:
                factor = jnp.where(below > i, factor, 0.0)
            blocks[b] = blocks[b] - factor * scaled
    work = jnp.concatenate(blocks, 0)
    pivots = jnp.sum(jnp.where(row_ids == col_ids, work[:, :n], 0.0), 1, keepdims=True)
    return work[:, n:] * lax.rsqrt(pivots)


def finish_kernel(where_ref, own_ref, other_ref, q_ref, merged_hbm, new_ref, q_next_ref, stack_ref, merged_ref, sem):
    load = pltpu.make_async_copy(merged_hbm, merged_ref, sem)
    load.start()
    chunks, rows, lanes = own_ref.shape
    units, rank = 2 * rows, q_ref.shape[1]
    first = where_ref[0] == 0
    for j in range(chunks):
        at = slice(j * lanes, (j + 1) * lanes)
        stack_ref[0:rows, at] = jnp.where(first, own_ref[j], other_ref[j])
        stack_ref[rows:units, at] = jnp.where(first, other_ref[j], own_ref[j])
    q_gate = jnp.concatenate(three_parts(q_ref[0]), 0)
    q_up = jnp.concatenate(three_parts(q_ref[1]), 0)
    width = chunks * lanes
    step = 1024
    for f in range(0, width, step):
        p_parts = jnp.dot(q_gate, stack_ref[0:rows, f : f + step], preferred_element_type=jnp.float32)
        p_parts += jnp.dot(q_up, stack_ref[rows:units, f : f + step], preferred_element_type=jnp.float32)
        p_mean = p_parts[0:rank] + p_parts[rank : 2 * rank] + p_parts[2 * rank :]
        for k, part in enumerate(three_parts(p_mean)):
            stack_ref[units + k * rank : units + (k + 1) * rank, f : f + step] = part
    products = lax.dot_general(
        stack_ref[...], stack_ref[units:, :], (((1,), (1,)), ((), ())), preferred_element_type=jnp.float32
    )
    products = products[:, 0:rank] + products[:, rank : 2 * rank] + products[:, 2 * rank :]
    gram = products[units : units + rank] + products[units + rank : units + 2 * rank] + products[units + 2 * rank :]
    inverse = inverse_cholesky(gram)
    for k in range(2):
        q_next_ref[k] = lax.dot_general(
            inverse, products[k * rows : (k + 1) * rows], (((1,), (1,)), ((), ())),
            precision=HIGH_PRECISION, preferred_element_type=jnp.float32,
        )
    gram_inverse = jnp.dot(inverse.T, inverse, precision=HIGH_PRECISION, preferred_element_type=jnp.float32)
    weights = jnp.dot(
        products[0:units], gram_inverse, precision=HIGH_PRECISION, preferred_element_type=jnp.float32
    )
    high, middle, _ = three_parts(weights)
    factors = jnp.concatenate([high, high, middle], 1)
    load.wait()
    for f in range(0, width, step):
        p_high = stack_ref[units : units + rank, f : f + step]
        p_middle = stack_ref[units + rank : units + 2 * rank, f : f + step]
        basis = jnp.concatenate([p_high, p_middle, p_high], 0)
        approximation = jnp.dot(factors, basis, preferred_element_type=jnp.float32)
        fresh = (merged_ref[:, f : f + step] - approximation).astype(jnp.bfloat16)
        new_ref[0, :, f : f + step] = fresh[0:rows]
        new_ref[1, :, f : f + step] = fresh[rows:]


def finish(where, own, other, q_prev, merged):
    rows = own.shape[1]
    width = own.shape[0] * own.shape[2]
    rank = q_prev.shape[2]
    vmem = pl.BlockSpec(memory_space=pltpu.VMEM)
    return pl.pallas_call(
        finish_kernel,
        out_shape=(
            jax.ShapeDtypeStruct((2, rows, width), jnp.bfloat16),
            jax.ShapeDtypeStruct((2, rank, rows), jnp.float32),
        ),
        in_specs=[pl.BlockSpec(memory_space=pltpu.SMEM), vmem, vmem, vmem, pl.BlockSpec(memory_space=pl.ANY)],
        out_specs=(vmem, vmem),
        scratch_shapes=[
            pltpu.VMEM((2 * rows + 3 * rank, width), jnp.bfloat16),
            pltpu.VMEM((2 * rows, width), jnp.float32),
            pltpu.SemaphoreType.DMA,
        ],
        compiler_params=pltpu.CompilerParams(vmem_limit_bytes=VMEM_BYTES),
        name="finish",
    )(where, own, other, q_prev.transpose(0, 2, 1), merged)


def shard_offset(tensor_index, shift, width, tensor_ways):
    shard = (tensor_index + shift + tensor_ways) % tensor_ways
    return pl.multiple_of(shard * width, width)


def add_products(pre, where_ref, gate_ref, up_ref, shards, shard_width, tensor_ways):
    for ref, shift, start in shards:
        at = shard_offset(where_ref[1], shift, shard_width, tensor_ways) + start
        at = pl.ds(pl.multiple_of(at, 128), ref.shape[1])
        weights = jnp.concatenate([gate_ref[:, at], up_ref[:, at]], 0)
        pre += lax.dot_general(weights, ref[...], (((1,), (1,)), ((), ())), preferred_element_type=jnp.float32)
    return pre


def early_kernel(where_ref, gate_ref, up_ref, *refs, shifts, tensor_ways):
    shards = [(ref, shift, 0) for ref, shift in zip(refs[:-1], shifts)]
    pre_ref = refs[-1]
    zeros = jnp.zeros(pre_ref.shape, jnp.float32)
    pre_ref[...] = add_products(zeros, where_ref, gate_ref, up_ref, shards, refs[0].shape[1], tensor_ways)


def early_products(where, w_gate, w_up, shards, tensor_ways):
    vmem = pl.BlockSpec(memory_space=pltpu.VMEM)
    return pl.pallas_call(
        functools.partial(early_kernel, shifts=[shift for _, shift in shards], tensor_ways=tensor_ways),
        out_shape=jax.ShapeDtypeStruct((2 * w_gate.shape[0], shards[0][0].shape[0]), jnp.float32),
        in_specs=[pl.BlockSpec(memory_space=pltpu.SMEM)] + [vmem] * (2 + len(shards)),
        out_specs=vmem,
        compiler_params=pltpu.CompilerParams(vmem_limit_bytes=VMEM_BYTES),
        name="early_products",
    )(where, w_gate, w_up, *[shard for shard, _ in shards])


def gradient_kernel(where_ref, pre_ref, gate_ref, up_ref, cot_ref, error_ref, *refs, places, early, shard_width, tensor_ways, scale):
    sources = refs[: len(places)]
    d_ref, send_ref, keep_ref, merged_ref, tokens_ref, sems = refs[len(places) :]
    rows = gate_ref.shape[0]
    lanes = send_ref.shape[2]
    slots = []
    column = 0
    for source, (shift, start) in zip(sources, places):
        slots.append((tokens_ref.at[:, pl.ds(column, source.shape[1])], shift, start))
        column += source.shape[1]
    order = list(range(early, len(places))) + list(range(early))
    copies = [pltpu.make_async_copy(sources[i], slots[i][0], sems.at[i]) for i in range(len(places))]
    for i in order:
        copies[i].start()
    pre = pre_ref[...]
    for i in order[: len(places) - early]:
        copies[i].wait()
        pre = add_products(pre, where_ref, gate_ref, up_ref, slots[i : i + 1], shard_width, tensor_ways)
    gate_pre, up_pre = pre[0:rows], pre[rows:]
    squash = jax.nn.sigmoid(gate_pre)
    upstream = cot_ref[...].astype(jnp.float32)
    d_gate = (upstream * up_pre * squash * (1.0 + gate_pre * (1.0 - squash))).astype(jnp.bfloat16)
    d_up = (upstream * gate_pre * squash).astype(jnp.bfloat16)
    d_both = jnp.concatenate([d_gate, d_up], 0)
    d_ref[...] = d_both
    first = where_ref[0] == 0
    for i in order:
        if i < early:
            copies[i].wait()
        ref, shift, start = slots[i]
        size = ref.shape[1]
        at = pl.multiple_of(shard_offset(where_ref[1], shift, shard_width, tensor_ways) + start, 128)
        grads = jnp.dot(d_both, ref[...], preferred_element_type=jnp.float32) * scale
        gate_half = grads[0:rows] + error_ref[0, :, pl.ds(at, size)].astype(jnp.float32)
        up_half = grads[rows:] + error_ref[1, :, pl.ds(at, size)].astype(jnp.float32)
        merged_ref[0:rows, pl.ds(at, size)] = gate_half
        merged_ref[rows:, pl.ds(at, size)] = up_half
        gate_half = gate_half.astype(jnp.bfloat16)
        up_half = up_half.astype(jnp.bfloat16)
        keep = jnp.where(first, gate_half, up_half)
        send = jnp.where(first, up_half, gate_half)
        chunk = at // lanes
        for k in range(size // lanes):
            part = slice(k * lanes, (k + 1) * lanes)
            keep_ref[chunk + k] = keep[:, part]
            send_ref[chunk + k] = send[:, part]


def gradients(where, pre, shards, early, w_gate, w_up, cot, error_fb, n_chips, tensor_ways):
    rows, width = w_gate.shape
    count = pre.shape[1]
    lanes = width // n_chips
    vmem = pl.BlockSpec(memory_space=pltpu.VMEM)
    here = pl.BlockSpec(memory_space=pl.ANY)
    whole_width = shards[0][0].shape[1]
    operands = [
        pltpu.with_memory_space_constraint(shard, pltpu.HBM) if shard.shape[1] == whole_width else shard
        for shard, _, _ in shards
    ]
    return pl.pallas_call(
        functools.partial(
            gradient_kernel,
            places=[(shift, start) for _, shift, start in shards],
            early=early,
            shard_width=width // tensor_ways,
            tensor_ways=tensor_ways,
            scale=1.0 / math.sqrt(count),
        ),
        out_shape=(
            jax.ShapeDtypeStruct((2 * rows, count), jnp.bfloat16),
            jax.ShapeDtypeStruct((n_chips, rows, lanes), jnp.bfloat16),
            jax.ShapeDtypeStruct((n_chips, rows, lanes), jnp.bfloat16),
            jax.ShapeDtypeStruct((2 * rows, width), jnp.float32),
        ),
        in_specs=[pl.BlockSpec(memory_space=pltpu.SMEM)] + [vmem] * 5 + [here] * len(shards),
        out_specs=(vmem,) * 4,
        scratch_shapes=[pltpu.VMEM((count, width), jnp.bfloat16), pltpu.SemaphoreType.DMA((len(shards),))],
        compiler_params=pltpu.CompilerParams(vmem_limit_bytes=VMEM_BYTES),
        name="gradients",
    )(where, pre, w_gate, w_up, cot.T, error_fb.reshape(2, rows, width), *operands)


def act_kernel(d_ref, gate_ref, up_ref, act_ref):
    d_both = d_ref[...].T
    step = 1024
    for f in range(0, act_ref.shape[1], step):
        at = slice(f, f + step)
        weights = jnp.concatenate([gate_ref[:, at], up_ref[:, at]], 0)
        act_ref[:, at] = jnp.dot(d_both, weights, preferred_element_type=jnp.float32).astype(jnp.bfloat16)


def act_terms(d_both, w_gate, w_up):
    vmem = pl.BlockSpec(memory_space=pltpu.VMEM)
    return pl.pallas_call(
        act_kernel,
        out_shape=jax.ShapeDtypeStruct((d_both.shape[1], w_gate.shape[1]), jnp.bfloat16),
        in_specs=[vmem] * 3,
        out_specs=vmem,
        compiler_params=pltpu.CompilerParams(vmem_limit_bytes=VMEM_BYTES),
        name="act_terms",
    )(d_both, w_gate, w_up)


def mean_kernel(pieces_ref, copies_ref, *, scale):
    total = pieces_ref[0].astype(jnp.float32)
    for k in range(1, pieces_ref.shape[0]):
        total += pieces_ref[k].astype(jnp.float32)
    mean = (total * scale).astype(jnp.bfloat16)
    for k in range(copies_ref.shape[0]):
        copies_ref[k] = mean


def mean_copies(pieces, workers):
    vmem = pl.BlockSpec(memory_space=pltpu.VMEM)
    return pl.pallas_call(
        functools.partial(mean_kernel, scale=1.0 / workers),
        out_shape=jax.ShapeDtypeStruct(pieces.shape, jnp.bfloat16),
        in_specs=[vmem],
        out_specs=vmem,
        compiler_params=pltpu.CompilerParams(vmem_limit_bytes=VMEM_BYTES),
        name="mean_copies",
    )(pieces)


def ring(value, step):
    ways = lax.axis_size("tensor")
    return lax.ppermute(value, "tensor", [(i, (i + step) % ways) for i in range(ways)])


def on_device(tokens, w_gate, w_up, d_hidden, error_fb, q_prev):
    core = lax.axis_index("core")
    n_chips = lax.axis_size(CHIPS)
    ways = lax.axis_size("tensor")
    where = jnp.stack([core, lax.axis_index("tensor")])
    share = w_gate.shape[1] // ways

    shards = [(tokens, 0, 0)]
    ahead = behind = tokens
    for k in range(1, ways // 2):
        ahead, behind = ring(ahead, 1), ring(behind, -1)
        shards += [(ahead, -k, 0), (behind, k, 0)]
    early = 5
    pre = early_products(where, w_gate, w_up, [shard[:2] for shard in shards[:early]], ways)
    middle = share // 2
    ahead, behind, pre = lax.optimization_barrier((ahead[:, :middle], behind[:, middle:], pre))
    shards += [(ring(ahead, 1), ways // 2, 0), (ring(behind, -1), ways // 2, middle)]
    d_both, send, keep, merged = gradients(
        where, pre, shards, early, w_gate, w_up, d_hidden, error_fb, n_chips, ways
    )
    act = act_terms(d_both, w_gate, w_up)
    got = lax.ppermute(send, "core", SWAP)
    pieces = (keep.astype(jnp.float32) + got.astype(jnp.float32)).astype(jnp.bfloat16)
    pieces, act = lax.optimization_barrier((pieces, act))
    d_tokens = lax.psum_scatter(act, "tensor", scatter_dimension=1, tiled=True)
    pieces = lax.all_to_all(pieces, CHIPS, 0, 0, tiled=True)
    copies = mean_copies(pieces, n_chips * lax.axis_size("core"))
    own_half = lax.all_to_all(copies, CHIPS, 0, 0, tiled=True)
    other_half = lax.ppermute(own_half, "core", SWAP)
    new_error, q_next = finish(where, own_half, other_half, q_prev, merged)
    return (d_tokens, new_error.reshape(error_fb.shape), q_next.transpose(0, 2, 1))


def solution(mesh):
    chips_apart = Mesh(mesh.devices.reshape(4, 8, 2, 8), ("x", "z", "core", "tensor"))
    dp = ("x", "z", "core")
    return jax.shard_map(
        on_device,
        mesh=chips_apart,
        in_specs=(
            P(dp, "tensor"),
            P("tensor", None),
            P("tensor", None),
            P(dp, "tensor"),
            P(dp, None, "tensor", None),
            P(None, "tensor", None),
        ),
        out_specs=(P(dp, "tensor"), P(dp, None, "tensor", None), P(None, "tensor", None)),
        check_vma=False,
    )
```

```python
import functools
import math

import jax
import jax.numpy as jnp
from jax import lax
from jax.experimental import pallas as pl
from jax.experimental.pallas import tpu as pltpu
from jax.sharding import Mesh, PartitionSpec as P

HIGH_PRECISION = lax.Precision.HIGHEST
CHIPS = ("x", "z")
SWAP = ((0, 1), (1, 0))
VMEM_BYTES = 24 * 1024 * 1024


def three_parts(value):
    high = value.astype(jnp.bfloat16)
    rest = value - high.astype(jnp.float32)
    middle = rest.astype(jnp.bfloat16)
    low = (rest - middle.astype(jnp.float32)).astype(jnp.bfloat16)
    return high, middle, low


def inverse_cholesky(gram):
    n = gram.shape[0]
    row_ids = lax.broadcasted_iota(jnp.int32, (n, n), 0)
    col_ids = lax.broadcasted_iota(jnp.int32, (n, n), 1)
    work = jnp.concatenate([gram, jnp.where(row_ids == col_ids, 1.0, 0.0)], 1)
    blocks = [work[8 * k : 8 * k + 8] for k in range(n // 8)]
    below = lax.broadcasted_iota(jnp.int32, (8, 2 * n), 0)
    for j in range(0, n - 2, 2):
        k, i = divmod(j, 8)
        upper, lower = blocks[k][i : i + 1], blocks[k][i + 1 : i + 2]
        a, b, c = upper[:, j : j + 1], upper[:, j + 1 : j + 2], lower[:, j + 1 : j + 2]
        shrink = 1.0 / (a * c - b * b)
        first = (c * upper - b * lower) * shrink
        second = (a * lower - b * upper) * shrink
        for m in range(k, n // 8):
            left = jnp.broadcast_to(blocks[m][:, j : j + 1], (8, 2 * n))
            right = jnp.broadcast_to(blocks[m][:, j + 1 : j + 2], (8, 2 * n))
            change = left * first + right * second
            if m == k:
                change = jnp.where(below > i + 1, change, 0.0)
            blocks[m] = blocks[m] - change
    work = jnp.concatenate(blocks, 0)
    pivots, rows = work[:, :n], work[:, n:]
    odd = (row_ids[:, 0:1] & 1) == 1
    diagonal = jnp.sum(jnp.where(row_ids == col_ids, pivots, 0.0), 1, keepdims=True)
    beside = jnp.sum(jnp.where(row_ids == col_ids + 1, pivots, 0.0), 1, keepdims=True)
    ratio = jnp.where(odd, beside / pltpu.roll(diagonal, 1, 0), 0.0)
    return (rows - ratio * pltpu.roll(rows, 1, 0)) * lax.rsqrt(diagonal - ratio * beside)


def finish_kernel(where_ref, own_ref, other_ref, q_ref, merged_hbm, new_ref, q_next_ref, stack_ref, merged_ref, sem):
    load = pltpu.make_async_copy(merged_hbm, merged_ref, sem)
    load.start()
    chunks, rows, lanes = own_ref.shape
    units, rank = 2 * rows, q_ref.shape[0]
    first = where_ref[0] == 0
    for j in range(chunks):
        at = slice(j * lanes, (j + 1) * lanes)
        stack_ref[0:rows, at] = jnp.where(first, own_ref[j], other_ref[j])
        stack_ref[rows:units, at] = jnp.where(first, other_ref[j], own_ref[j])
    q_parts = jnp.concatenate(three_parts(q_ref[...]), 0)
    width = chunks * lanes
    step = 1024
    for f in range(0, width, step):
        p_parts = jnp.dot(q_parts, stack_ref[0:units, f : f + step], preferred_element_type=jnp.float32)
        p_mean = p_parts[0:rank] + p_parts[rank : 2 * rank] + p_parts[2 * rank :]
        for k, part in enumerate(three_parts(p_mean)):
            stack_ref[units + k * rank : units + (k + 1) * rank, f : f + step] = part
    products = lax.dot_general(
        stack_ref[...], stack_ref[units:, :], (((1,), (1,)), ((), ())), preferred_element_type=jnp.float32
    )
    products = products[:, 0:rank] + products[:, rank : 2 * rank] + products[:, 2 * rank :]
    gram = products[units : units + rank] + products[units + rank : units + 2 * rank] + products[units + 2 * rank :]
    inverse = inverse_cholesky(gram)
    for k in range(2):
        q_next_ref[k] = lax.dot_general(
            inverse, products[k * rows : (k + 1) * rows], (((1,), (1,)), ((), ())),
            precision=HIGH_PRECISION, preferred_element_type=jnp.float32,
        )
    gram_inverse = jnp.dot(inverse.T, inverse, precision=HIGH_PRECISION, preferred_element_type=jnp.float32)
    weights = jnp.dot(
        products[0:units], gram_inverse, precision=HIGH_PRECISION, preferred_element_type=jnp.float32
    )
    high, middle, _ = three_parts(weights)
    factors = jnp.concatenate([high, high, middle], 1)
    load.wait()
    for f in range(0, width, step):
        p_high = stack_ref[units : units + rank, f : f + step]
        p_middle = stack_ref[units + rank : units + 2 * rank, f : f + step]
        basis = jnp.concatenate([p_high, p_middle, p_high], 0)
        approximation = jnp.dot(factors, basis, preferred_element_type=jnp.float32)
        fresh = (merged_ref[:, f : f + step] - approximation).astype(jnp.bfloat16)
        new_ref[0, :, f : f + step] = fresh[0:rows]
        new_ref[1, :, f : f + step] = fresh[rows:]


def finish(where, own, other, q_prev, merged):
    rows = own.shape[1]
    width = own.shape[0] * own.shape[2]
    rank = q_prev.shape[2]
    vmem = pl.BlockSpec(memory_space=pltpu.VMEM)
    return pl.pallas_call(
        finish_kernel,
        out_shape=(
            jax.ShapeDtypeStruct((2, rows, width), jnp.bfloat16),
            jax.ShapeDtypeStruct((2, rank, rows), jnp.float32),
        ),
        in_specs=[pl.BlockSpec(memory_space=pltpu.SMEM), vmem, vmem, vmem, pl.BlockSpec(memory_space=pl.ANY)],
        out_specs=(vmem, vmem),
        scratch_shapes=[
            pltpu.VMEM((2 * rows + 3 * rank, width), jnp.bfloat16),
            pltpu.VMEM((2 * rows, width), jnp.float32),
            pltpu.SemaphoreType.DMA,
        ],
        compiler_params=pltpu.CompilerParams(vmem_limit_bytes=VMEM_BYTES),
        name="finish",
    )(where, own, other, q_prev.transpose(2, 0, 1).reshape(rank, 2 * rows), pltpu.with_memory_space_constraint(merged, pltpu.HBM))


def shard_offset(tensor_index, shift, start, shard_width, tensor_ways):
    shard = (tensor_index + shift + tensor_ways) % tensor_ways
    return pl.multiple_of(shard * shard_width + start, 128)


def add_products(pre, where_ref, gate_ref, up_ref, shards, shard_width, tensor_ways):
    for ref, shift, start in shards:
        at = pl.ds(shard_offset(where_ref[1], shift, start, shard_width, tensor_ways), ref.shape[1])
        weights = jnp.concatenate([gate_ref[:, at], up_ref[:, at]], 0)
        pre += lax.dot_general(weights, ref[...], (((1,), (1,)), ((), ())), preferred_element_type=jnp.float32)
    return pre


def early_kernel(where_ref, gate_ref, up_ref, *refs, shifts, shard_width, tensor_ways):
    shards = [(ref, shift, 0) for ref, shift in zip(refs[:-1], shifts)]
    pre_ref = refs[-1]
    zeros = jnp.zeros(pre_ref.shape, jnp.float32)
    pre_ref[...] = add_products(zeros, where_ref, gate_ref, up_ref, shards, shard_width, tensor_ways)


def early_products(where, w_gate, w_up, shards, tensor_ways):
    vmem = pl.BlockSpec(memory_space=pltpu.VMEM)
    return pl.pallas_call(
        functools.partial(
            early_kernel,
            shifts=[shift for _, shift in shards],
            shard_width=w_gate.shape[1] // tensor_ways,
            tensor_ways=tensor_ways,
        ),
        out_shape=jax.ShapeDtypeStruct((2 * w_gate.shape[0], shards[0][0].shape[0]), jnp.float32),
        in_specs=[pl.BlockSpec(memory_space=pltpu.SMEM)] + [vmem] * (2 + len(shards)),
        out_specs=vmem,
        compiler_params=pltpu.CompilerParams(vmem_limit_bytes=VMEM_BYTES),
        name="early_products",
    )(where, w_gate, w_up, *[shard for shard, _ in shards])


def gradient_kernel(where_ref, pre_ref, gate_ref, up_ref, cot_ref, error_ref, *refs, places, early, shard_width, tensor_ways, scale):
    sources = refs[: len(places)]
    d_ref, send_ref, keep_ref, merged_hbm, tokens_ref, send_buf, keep_buf, merged_ref, sems = refs[len(places) :]
    rows = gate_ref.shape[0]
    lanes = send_ref.shape[2]
    slots = []
    column = 0
    for source, (shift, start) in zip(sources, places):
        slots.append((tokens_ref.at[:, pl.ds(column, source.shape[1])], shift, start, column))
        column += source.shape[1]
    order = list(range(early, len(places))) + list(range(early))
    copies = [pltpu.make_async_copy(sources[i], slots[i][0], sems.at[i]) for i in range(len(places))]
    for i in order:
        copies[i].start()
    pre = pre_ref[...]
    for i in order[: len(places) - early]:
        copies[i].wait()
        pre = add_products(pre, where_ref, gate_ref, up_ref, [slots[i][:3]], shard_width, tensor_ways)
    gate_pre, up_pre = pre[0:rows], pre[rows:]
    squash = jax.nn.sigmoid(gate_pre)
    upstream = cot_ref[...].astype(jnp.float32)
    d_gate = (upstream * up_pre * squash * (1.0 + gate_pre * (1.0 - squash))).astype(jnp.bfloat16)
    d_up = (upstream * gate_pre * squash).astype(jnp.bfloat16)
    d_both = jnp.concatenate([d_gate, d_up], 0)
    d_ref[...] = d_both
    first = where_ref[0] == 0
    out = []
    for i in order:
        if i < early:
            copies[i].wait()
        ref, shift, start, column = slots[i]
        size = ref.shape[1]
        at = shard_offset(where_ref[1], shift, start, shard_width, tensor_ways)
        grads = jnp.dot(d_both, ref[...], preferred_element_type=jnp.float32) * scale
        gate_half = grads[0:rows] + error_ref[0, :, pl.ds(at, size)].astype(jnp.float32)
        up_half = grads[rows:] + error_ref[1, :, pl.ds(at, size)].astype(jnp.float32)
        merged_ref[0:rows, column : column + size] = gate_half
        merged_ref[rows:, column : column + size] = up_half
        gate_half = gate_half.astype(jnp.bfloat16)
        up_half = up_half.astype(jnp.bfloat16)
        keep = jnp.where(first, gate_half, up_half)
        send = jnp.where(first, up_half, gate_half)
        chunk, count = column // lanes, size // lanes
        for k in range(count):
            part = slice(k * lanes, (k + 1) * lanes)
            keep_buf[chunk + k] = keep[:, part]
            send_buf[chunk + k] = send[:, part]
        here, there = pl.ds(chunk, count), pl.ds(at // lanes, count)
        for source, target in (
            (send_buf.at[here], send_ref.at[there]),
            (keep_buf.at[here], keep_ref.at[there]),
            (merged_ref.at[:, pl.ds(column, size)], merged_hbm.at[:, pl.ds(at, size)]),
        ):
            copy = pltpu.make_async_copy(source, target, sems.at[len(places) + len(out)])
            copy.start()
            out.append(copy)
    for copy in out:
        copy.wait()


def gradients(where, pre, shards, early, w_gate, w_up, cot, error_fb, n_chips, tensor_ways):
    rows, width = w_gate.shape
    count = pre.shape[1]
    lanes = width // n_chips
    vmem = pl.BlockSpec(memory_space=pltpu.VMEM)
    here = pl.BlockSpec(memory_space=pl.ANY)
    last = 2
    operands = [pltpu.with_memory_space_constraint(shard, pltpu.HBM) for shard, _, _ in shards[:-last]]
    operands += [shard for shard, _, _ in shards[-last:]]
    return pl.pallas_call(
        functools.partial(
            gradient_kernel,
            places=[(shift, start) for _, shift, start in shards],
            early=early,
            shard_width=width // tensor_ways,
            tensor_ways=tensor_ways,
            scale=1.0 / math.sqrt(count),
        ),
        out_shape=(
            jax.ShapeDtypeStruct((2 * rows, count), jnp.bfloat16),
            pltpu.HBM((n_chips, rows, lanes), jnp.bfloat16),
            pltpu.HBM((n_chips, rows, lanes), jnp.bfloat16),
            pltpu.HBM((2 * rows, width), jnp.float32),
        ),
        in_specs=[pl.BlockSpec(memory_space=pltpu.SMEM)] + [vmem] * 5 + [here] * len(shards),
        out_specs=(vmem, here, here, here),
        scratch_shapes=[
            pltpu.VMEM((count, width), jnp.bfloat16),
            pltpu.VMEM((n_chips, rows, lanes), jnp.bfloat16),
            pltpu.VMEM((n_chips, rows, lanes), jnp.bfloat16),
            pltpu.VMEM((2 * rows, width), jnp.float32),
            pltpu.SemaphoreType.DMA((4 * len(shards),)),
        ],
        compiler_params=pltpu.CompilerParams(vmem_limit_bytes=VMEM_BYTES),
        name="gradients",
    )(where, pre, w_gate, w_up, cot.T, error_fb.reshape(2, rows, width), *operands)


def act_kernel(d_ref, gate_ref, up_ref, act_ref):
    d_both = d_ref[...].T
    step = 1024
    for f in range(0, act_ref.shape[1], step):
        at = slice(f, f + step)
        weights = jnp.concatenate([gate_ref[:, at], up_ref[:, at]], 0)
        act_ref[:, at] = jnp.dot(d_both, weights, preferred_element_type=jnp.float32).astype(jnp.bfloat16)


def act_terms(d_both, w_gate, w_up):
    vmem = pl.BlockSpec(memory_space=pltpu.VMEM)
    return pl.pallas_call(
        act_kernel,
        out_shape=jax.ShapeDtypeStruct((d_both.shape[1], w_gate.shape[1]), jnp.bfloat16),
        in_specs=[vmem] * 3,
        out_specs=vmem,
        compiler_params=pltpu.CompilerParams(vmem_limit_bytes=VMEM_BYTES),
        name="act_terms",
    )(d_both, w_gate, w_up)


def pair_kernel(keep_hbm, got_hbm, sum_ref, keep_ref, got_ref, sems):
    parts = sems.shape[1]
    step = sum_ref.shape[0] // parts

    def load(k):
        at = pl.ds(k * step, step)
        return (
            pltpu.make_async_copy(keep_hbm.at[at], keep_ref.at[at], sems.at[0, k]),
            pltpu.make_async_copy(got_hbm.at[at], got_ref.at[at], sems.at[1, k]),
        )

    for k in range(parts):
        for copy in load(k):
            copy.start()
    for k in range(parts):
        for copy in load(k):
            copy.wait()
        for i in range(k * step, (k + 1) * step):
            total = keep_ref[i].astype(jnp.float32) + got_ref[i].astype(jnp.float32)
            sum_ref[i] = total.astype(jnp.bfloat16)


def pair_sum(keep, got):
    vmem = pl.BlockSpec(memory_space=pltpu.VMEM)
    here = pl.BlockSpec(memory_space=pl.ANY)
    return pl.pallas_call(
        pair_kernel,
        out_shape=jax.ShapeDtypeStruct(keep.shape, jnp.bfloat16),
        in_specs=[here] * 2,
        out_specs=vmem,
        scratch_shapes=[
            pltpu.VMEM(keep.shape, jnp.bfloat16),
            pltpu.VMEM(keep.shape, jnp.bfloat16),
            pltpu.SemaphoreType.DMA((2, 4)),
        ],
        compiler_params=pltpu.CompilerParams(vmem_limit_bytes=VMEM_BYTES),
        name="pair_sum",
    )(pltpu.with_memory_space_constraint(keep, pltpu.HBM), got)


def mean_kernel(pieces_ref, copies_ref, *, scale):
    total = pieces_ref[0].astype(jnp.float32)
    for k in range(1, pieces_ref.shape[0]):
        total += pieces_ref[k].astype(jnp.float32)
    mean = (total * scale).astype(jnp.bfloat16)
    for k in range(copies_ref.shape[0]):
        copies_ref[k] = mean


def mean_copies(pieces, workers):
    vmem = pl.BlockSpec(memory_space=pltpu.VMEM)
    return pl.pallas_call(
        functools.partial(mean_kernel, scale=1.0 / workers),
        out_shape=jax.ShapeDtypeStruct(pieces.shape, jnp.bfloat16),
        in_specs=[vmem],
        out_specs=vmem,
        compiler_params=pltpu.CompilerParams(vmem_limit_bytes=VMEM_BYTES),
        name="mean_copies",
    )(pieces)


def ring(value, step):
    ways = lax.axis_size("tensor")
    return lax.ppermute(value, "tensor", [(i, (i + step) % ways) for i in range(ways)])


def on_device(tokens, w_gate, w_up, d_hidden, error_fb, q_prev):
    core = lax.axis_index("core")
    n_chips = lax.axis_size(CHIPS)
    ways = lax.axis_size("tensor")
    where = jnp.stack([core, lax.axis_index("tensor")])
    share = w_gate.shape[1] // ways

    shards = [(tokens, 0, 0)]
    ahead = behind = tokens
    for k in range(1, ways // 2):
        ahead, behind = ring(ahead, 1), ring(behind, -1)
        shards += [(ahead, -k, 0), (behind, k, 0)]
    early = 5
    pre = early_products(where, w_gate, w_up, [shard[:2] for shard in shards[:early]], ways)
    middle = share // 2
    ahead, behind, pre = lax.optimization_barrier((ahead[:, :middle], behind[:, middle:], pre))
    shards += [(ring(ahead, 1), ways // 2, 0), (ring(behind, -1), ways // 2, middle)]
    d_both, send, keep, merged = gradients(
        where, pre, shards, early, w_gate, w_up, d_hidden, error_fb, n_chips, ways
    )
    act = act_terms(d_both, w_gate, w_up)
    got = lax.ppermute(send, "core", SWAP)
    pieces = pair_sum(keep, got)
    pieces, act = lax.optimization_barrier((pieces, act))
    d_tokens = lax.psum_scatter(act, "tensor", scatter_dimension=1, tiled=True)
    pieces = lax.all_to_all(pieces, CHIPS, 0, 0, tiled=True)
    copies = mean_copies(pieces, n_chips * lax.axis_size("core"))
    own_half = lax.all_to_all(copies, CHIPS, 0, 0, tiled=True)
    other_half = lax.ppermute(own_half, "core", SWAP)
    new_error, q_next = finish(where, own_half, other_half, q_prev, merged)
    return (d_tokens, new_error.reshape(error_fb.shape), q_next.transpose(0, 2, 1))


def solution(mesh):
    chips_apart = Mesh(mesh.devices.reshape(4, 8, 2, 8), ("x", "z", "core", "tensor"))
    dp = ("x", "z", "core")
    return jax.shard_map(
        on_device,
        mesh=chips_apart,
        in_specs=(
            P(dp, "tensor"),
            P("tensor", None),
            P("tensor", None),
            P(dp, "tensor"),
            P(dp, None, "tensor", None),
            P(None, "tensor", None),
        ),
        out_specs=(P(dp, "tensor"), P(dp, None, "tensor", None), P(None, "tensor", None)),
        check_vma=False,
    )
```

```python
import functools
import math

import jax
import jax.numpy as jnp
from jax import lax
from jax.experimental import pallas as pl
from jax.experimental.pallas import tpu as pltpu
from jax.sharding import Mesh, PartitionSpec as P

HIGH_PRECISION = lax.Precision.HIGHEST
CHIPS = ("x", "z")
SWAP = ((0, 1), (1, 0))
VMEM_BYTES = 24 * 1024 * 1024


def three_parts(value):
    high = value.astype(jnp.bfloat16)
    rest = value - high.astype(jnp.float32)
    middle = rest.astype(jnp.bfloat16)
    low = (rest - middle.astype(jnp.float32)).astype(jnp.bfloat16)
    return high, middle, low


def inverse_cholesky(gram):
    n = gram.shape[0]
    row_ids = lax.broadcasted_iota(jnp.int32, (n, n), 0)
    col_ids = lax.broadcasted_iota(jnp.int32, (n, n), 1)
    work = jnp.concatenate([gram, jnp.where(row_ids == col_ids, 1.0, 0.0)], 1)
    blocks = [work[8 * k : 8 * k + 8] for k in range(n // 8)]
    below = lax.broadcasted_iota(jnp.int32, (8, 2 * n), 0)
    for j in range(0, n - 2, 2):
        k, i = divmod(j, 8)
        upper, lower = blocks[k][i : i + 1], blocks[k][i + 1 : i + 2]
        a, b, c = upper[:, j : j + 1], upper[:, j + 1 : j + 2], lower[:, j + 1 : j + 2]
        shrink = 1.0 / (a * c - b * b)
        first = (c * upper - b * lower) * shrink
        second = (a * lower - b * upper) * shrink
        for m in range(k, n // 8):
            left = jnp.broadcast_to(blocks[m][:, j : j + 1], (8, 2 * n))
            right = jnp.broadcast_to(blocks[m][:, j + 1 : j + 2], (8, 2 * n))
            change = left * first + right * second
            if m == k:
                change = jnp.where(below > i + 1, change, 0.0)
            blocks[m] = blocks[m] - change
    work = jnp.concatenate(blocks, 0)
    pivots, rows = work[:, :n], work[:, n:]
    odd = (row_ids[:, 0:1] & 1) == 1
    diagonal = jnp.sum(jnp.where(row_ids == col_ids, pivots, 0.0), 1, keepdims=True)
    beside = jnp.sum(jnp.where(row_ids == col_ids + 1, pivots, 0.0), 1, keepdims=True)
    ratio = jnp.where(odd, beside / pltpu.roll(diagonal, 1, 0), 0.0)
    return (rows - ratio * pltpu.roll(rows, 1, 0)) * lax.rsqrt(diagonal - ratio * beside)


def finish_kernel(where_ref, own_ref, other_ref, q_ref, merged_hbm, new_hbm, q_next_ref, stack_ref, merged_ref, new_ref, sem, out_sems):
    load = pltpu.make_async_copy(merged_hbm, merged_ref, sem)
    load.start()
    chunks, rows, lanes = own_ref.shape
    units, rank = 2 * rows, q_ref.shape[0]
    first = where_ref[0] == 0
    for j in range(chunks):
        at = slice(j * lanes, (j + 1) * lanes)
        stack_ref[0:rows, at] = jnp.where(first, own_ref[j], other_ref[j])
        stack_ref[rows:units, at] = jnp.where(first, other_ref[j], own_ref[j])
    q_parts = jnp.concatenate(three_parts(q_ref[...]), 0)
    width = chunks * lanes
    step = 1024
    for f in range(0, width, step):
        p_parts = jnp.dot(q_parts, stack_ref[0:units, f : f + step], preferred_element_type=jnp.float32)
        p_mean = p_parts[0:rank] + p_parts[rank : 2 * rank] + p_parts[2 * rank :]
        for k, part in enumerate(three_parts(p_mean)):
            stack_ref[units + k * rank : units + (k + 1) * rank, f : f + step] = part
    products = lax.dot_general(
        stack_ref[...], stack_ref[units:, :], (((1,), (1,)), ((), ())), preferred_element_type=jnp.float32
    )
    products = products[:, 0:rank] + products[:, rank : 2 * rank] + products[:, 2 * rank :]
    gram = products[units : units + rank] + products[units + rank : units + 2 * rank] + products[units + 2 * rank :]
    inverse = inverse_cholesky(gram)
    for k in range(2):
        q_next_ref[k] = lax.dot_general(
            inverse, products[k * rows : (k + 1) * rows], (((1,), (1,)), ((), ())),
            precision=HIGH_PRECISION, preferred_element_type=jnp.float32,
        )
    gram_inverse = jnp.dot(inverse.T, inverse, precision=HIGH_PRECISION, preferred_element_type=jnp.float32)
    weights = jnp.dot(
        products[0:units], gram_inverse, precision=HIGH_PRECISION, preferred_element_type=jnp.float32
    )
    high, middle, _ = three_parts(weights)
    factors = jnp.concatenate([high, high, middle], 1)
    load.wait()
    out = []
    for f in range(0, width, step):
        p_high = stack_ref[units : units + rank, f : f + step]
        p_middle = stack_ref[units + rank : units + 2 * rank, f : f + step]
        basis = jnp.concatenate([p_high, p_middle, p_high], 0)
        approximation = jnp.dot(factors, basis, preferred_element_type=jnp.float32)
        fresh = (merged_ref[:, f : f + step] - approximation).astype(jnp.bfloat16)
        new_ref[0, :, f : f + step] = fresh[0:rows]
        new_ref[1, :, f : f + step] = fresh[rows:]
        at = (slice(None), slice(None), pl.ds(f, step))
        copy = pltpu.make_async_copy(new_ref.at[at], new_hbm.at[at], out_sems.at[f // step])
        copy.start()
        out.append(copy)
    for copy in out:
        copy.wait()


def finish(where, own, other, q_prev, merged):
    rows = own.shape[1]
    width = own.shape[0] * own.shape[2]
    rank = q_prev.shape[2]
    vmem = pl.BlockSpec(memory_space=pltpu.VMEM)
    return pl.pallas_call(
        finish_kernel,
        out_shape=(
            jax.ShapeDtypeStruct((2, rows, width), jnp.bfloat16),
            jax.ShapeDtypeStruct((2, rank, rows), jnp.float32),
        ),
        in_specs=[pl.BlockSpec(memory_space=pltpu.SMEM), vmem, vmem, vmem, pl.BlockSpec(memory_space=pl.ANY)],
        out_specs=(pl.BlockSpec(memory_space=pl.ANY), vmem),
        scratch_shapes=[
            pltpu.VMEM((2 * rows + 3 * rank, width), jnp.bfloat16),
            pltpu.VMEM((2 * rows, width), jnp.float32),
            pltpu.VMEM((2, rows, width), jnp.bfloat16),
            pltpu.SemaphoreType.DMA,
            pltpu.SemaphoreType.DMA((width // 1024,)),
        ],
        compiler_params=pltpu.CompilerParams(vmem_limit_bytes=VMEM_BYTES),
        name="finish",
    )(where, own, other, q_prev.transpose(2, 0, 1).reshape(rank, 2 * rows), pltpu.with_memory_space_constraint(merged, pltpu.HBM))


def shard_offset(tensor_index, shift, start, shard_width, tensor_ways):
    shard = (tensor_index + shift + tensor_ways) % tensor_ways
    return pl.multiple_of(shard * shard_width + start, 128)


def add_products(pre, where_ref, gate_ref, up_ref, shards, shard_width, tensor_ways):
    for ref, shift, start in shards:
        at = pl.ds(shard_offset(where_ref[1], shift, start, shard_width, tensor_ways), ref.shape[1])
        weights = jnp.concatenate([gate_ref[:, at], up_ref[:, at]], 0)
        pre += lax.dot_general(weights, ref[...], (((1,), (1,)), ((), ())), preferred_element_type=jnp.float32)
    return pre


def early_kernel(where_ref, gate_ref, up_ref, *refs, shifts, shard_width, tensor_ways):
    shards = [(ref, shift, 0) for ref, shift in zip(refs, shifts)]
    before, pre_ref = refs[len(shifts) : -1], refs[-1]
    start = before[0][...] if before else jnp.zeros(pre_ref.shape, jnp.float32)
    pre_ref[...] = add_products(start, where_ref, gate_ref, up_ref, shards, shard_width, tensor_ways)


def early_products(where, w_gate, w_up, shards, tensor_ways, before=()):
    vmem = pl.BlockSpec(memory_space=pltpu.VMEM)
    return pl.pallas_call(
        functools.partial(
            early_kernel,
            shifts=[shift for _, shift in shards],
            shard_width=w_gate.shape[1] // tensor_ways,
            tensor_ways=tensor_ways,
        ),
        out_shape=jax.ShapeDtypeStruct((2 * w_gate.shape[0], shards[0][0].shape[0]), jnp.float32),
        in_specs=[pl.BlockSpec(memory_space=pltpu.SMEM)] + [vmem] * (2 + len(shards) + len(before)),
        out_specs=vmem,
        compiler_params=pltpu.CompilerParams(vmem_limit_bytes=VMEM_BYTES),
        name="early_products",
    )(where, w_gate, w_up, *[shard for shard, _ in shards], *before)


def gradient_kernel(where_ref, pre_ref, gate_ref, up_ref, cot_ref, error_ref, *refs, places, early, shard_width, tensor_ways, scale):
    sources = refs[: len(places)]
    d_ref, send_ref, keep_ref, merged_hbm, tokens_ref, send_buf, keep_buf, merged_ref, sems = refs[len(places) :]
    rows = gate_ref.shape[0]
    lanes = send_ref.shape[2]
    slots = []
    column = 0
    for source, (shift, start) in zip(sources, places):
        slots.append((tokens_ref.at[:, pl.ds(column, source.shape[1])], shift, start, column))
        column += source.shape[1]
    order = list(range(early, len(places))) + list(range(early))
    copies = [pltpu.make_async_copy(sources[i], slots[i][0], sems.at[i]) for i in range(len(places))]
    for i in order:
        copies[i].start()
    pre = pre_ref[...]
    for i in order[: len(places) - early]:
        copies[i].wait()
        pre = add_products(pre, where_ref, gate_ref, up_ref, [slots[i][:3]], shard_width, tensor_ways)
    gate_pre, up_pre = pre[0:rows], pre[rows:]
    squash = jax.nn.sigmoid(gate_pre)
    upstream = cot_ref[...].astype(jnp.float32)
    d_gate = (upstream * up_pre * squash * (1.0 + gate_pre * (1.0 - squash))).astype(jnp.bfloat16)
    d_up = (upstream * gate_pre * squash).astype(jnp.bfloat16)
    d_both = jnp.concatenate([d_gate, d_up], 0)
    d_ref[...] = d_both
    first = where_ref[0] == 0
    out = []
    for i in order:
        if i < early:
            copies[i].wait()
        ref, shift, start, column = slots[i]
        size = ref.shape[1]
        at = shard_offset(where_ref[1], shift, start, shard_width, tensor_ways)
        grads = jnp.dot(d_both, ref[...], preferred_element_type=jnp.float32) * scale
        gate_half = grads[0:rows] + error_ref[0, :, pl.ds(at, size)].astype(jnp.float32)
        up_half = grads[rows:] + error_ref[1, :, pl.ds(at, size)].astype(jnp.float32)
        merged_ref[0:rows, column : column + size] = gate_half
        merged_ref[rows:, column : column + size] = up_half
        gate_half = gate_half.astype(jnp.bfloat16)
        up_half = up_half.astype(jnp.bfloat16)
        keep = jnp.where(first, gate_half, up_half)
        send = jnp.where(first, up_half, gate_half)
        chunk, count = column // lanes, size // lanes
        for k in range(count):
            part = slice(k * lanes, (k + 1) * lanes)
            keep_buf[chunk + k] = keep[:, part]
            send_buf[chunk + k] = send[:, part]
        here, there = pl.ds(chunk, count), pl.ds(at // lanes, count)
        for source, target in (
            (send_buf.at[here], send_ref.at[there]),
            (keep_buf.at[here], keep_ref.at[there]),
            (merged_ref.at[:, pl.ds(column, size)], merged_hbm.at[:, pl.ds(at, size)]),
        ):
            copy = pltpu.make_async_copy(source, target, sems.at[len(places) + len(out)])
            copy.start()
            out.append(copy)
    for copy in out:
        copy.wait()


def gradients(where, pre, shards, early, w_gate, w_up, cot, error_fb, n_chips, tensor_ways):
    rows, width = w_gate.shape
    count = pre.shape[1]
    lanes = width // n_chips
    vmem = pl.BlockSpec(memory_space=pltpu.VMEM)
    here = pl.BlockSpec(memory_space=pl.ANY)
    last = 2
    operands = [pltpu.with_memory_space_constraint(shard, pltpu.HBM) for shard, _, _ in shards[:-last]]
    operands += [shard for shard, _, _ in shards[-last:]]
    return pl.pallas_call(
        functools.partial(
            gradient_kernel,
            places=[(shift, start) for _, shift, start in shards],
            early=early,
            shard_width=width // tensor_ways,
            tensor_ways=tensor_ways,
            scale=1.0 / math.sqrt(count),
        ),
        out_shape=(
            jax.ShapeDtypeStruct((2 * rows, count), jnp.bfloat16),
            pltpu.HBM((n_chips, rows, lanes), jnp.bfloat16),
            pltpu.HBM((n_chips, rows, lanes), jnp.bfloat16),
            pltpu.HBM((2 * rows, width), jnp.float32),
        ),
        in_specs=[pl.BlockSpec(memory_space=pltpu.SMEM)] + [vmem] * 5 + [here] * len(shards),
        out_specs=(vmem, here, here, here),
        scratch_shapes=[
            pltpu.VMEM((count, width), jnp.bfloat16),
            pltpu.VMEM((n_chips, rows, lanes), jnp.bfloat16),
            pltpu.VMEM((n_chips, rows, lanes), jnp.bfloat16),
            pltpu.VMEM((2 * rows, width), jnp.float32),
            pltpu.SemaphoreType.DMA((4 * len(shards),)),
        ],
        compiler_params=pltpu.CompilerParams(vmem_limit_bytes=VMEM_BYTES),
        name="gradients",
    )(where, pre, w_gate, w_up, cot.T, error_fb.reshape(2, rows, width), *operands)


def act_kernel(d_ref, gate_ref, up_ref, act_ref):
    d_both = d_ref[...].T
    step = 1024
    for f in range(0, act_ref.shape[1], step):
        at = slice(f, f + step)
        weights = jnp.concatenate([gate_ref[:, at], up_ref[:, at]], 0)
        act_ref[:, at] = jnp.dot(d_both, weights, preferred_element_type=jnp.float32).astype(jnp.bfloat16)


def act_terms(d_both, w_gate, w_up):
    vmem = pl.BlockSpec(memory_space=pltpu.VMEM)
    return pl.pallas_call(
        act_kernel,
        out_shape=jax.ShapeDtypeStruct((d_both.shape[1], w_gate.shape[1]), jnp.bfloat16),
        in_specs=[vmem] * 3,
        out_specs=vmem,
        compiler_params=pltpu.CompilerParams(vmem_limit_bytes=VMEM_BYTES),
        name="act_terms",
    )(d_both, w_gate, w_up)


def pair_kernel(keep_hbm, got_hbm, sum_ref, keep_ref, got_ref, sems):
    parts = sems.shape[1]
    step = sum_ref.shape[0] // parts

    def load(k):
        at = pl.ds(k * step, step)
        return (
            pltpu.make_async_copy(keep_hbm.at[at], keep_ref.at[at], sems.at[0, k]),
            pltpu.make_async_copy(got_hbm.at[at], got_ref.at[at], sems.at[1, k]),
        )

    for k in range(parts):
        for copy in load(k):
            copy.start()
    for k in range(parts):
        for copy in load(k):
            copy.wait()
        for i in range(k * step, (k + 1) * step):
            total = keep_ref[i].astype(jnp.float32) + got_ref[i].astype(jnp.float32)
            sum_ref[i] = total.astype(jnp.bfloat16)


def pair_sum(keep, got):
    vmem = pl.BlockSpec(memory_space=pltpu.VMEM)
    here = pl.BlockSpec(memory_space=pl.ANY)
    return pl.pallas_call(
        pair_kernel,
        out_shape=jax.ShapeDtypeStruct(keep.shape, jnp.bfloat16),
        in_specs=[here] * 2,
        out_specs=vmem,
        scratch_shapes=[
            pltpu.VMEM(keep.shape, jnp.bfloat16),
            pltpu.VMEM(keep.shape, jnp.bfloat16),
            pltpu.SemaphoreType.DMA((2, 4)),
        ],
        compiler_params=pltpu.CompilerParams(vmem_limit_bytes=VMEM_BYTES),
        name="pair_sum",
    )(pltpu.with_memory_space_constraint(keep, pltpu.HBM), got)


def mean_kernel(pieces_ref, copies_ref, *, scale):
    total = pieces_ref[0].astype(jnp.float32)
    for k in range(1, pieces_ref.shape[0]):
        total += pieces_ref[k].astype(jnp.float32)
    mean = (total * scale).astype(jnp.bfloat16)
    for k in range(copies_ref.shape[0]):
        copies_ref[k] = mean


def mean_copies(pieces, workers):
    vmem = pl.BlockSpec(memory_space=pltpu.VMEM)
    return pl.pallas_call(
        functools.partial(mean_kernel, scale=1.0 / workers),
        out_shape=jax.ShapeDtypeStruct(pieces.shape, jnp.bfloat16),
        in_specs=[vmem],
        out_specs=vmem,
        compiler_params=pltpu.CompilerParams(vmem_limit_bytes=VMEM_BYTES),
        name="mean_copies",
    )(pieces)


def ring(value, step):
    ways = lax.axis_size("tensor")
    return lax.ppermute(value, "tensor", [(i, (i + step) % ways) for i in range(ways)])


def on_device(tokens, w_gate, w_up, d_hidden, error_fb, q_prev):
    core = lax.axis_index("core")
    n_chips = lax.axis_size(CHIPS)
    ways = lax.axis_size("tensor")
    where = jnp.stack([core, lax.axis_index("tensor")])
    share = w_gate.shape[1] // ways

    shards = [(tokens, 0, 0)]
    ahead = behind = tokens
    for k in range(1, ways // 2):
        ahead, behind = ring(ahead, 1), ring(behind, -1)
        shards += [(ahead, -k, 0), (behind, k, 0)]
    early = 5
    pre = early_products(where, w_gate, w_up, [shard[:2] for shard in shards[:early]], ways)
    middle = share * 3 // 4
    ahead, behind, pre = lax.optimization_barrier((ahead[:, :middle], behind[:, middle:], pre))
    pre = early_products(where, w_gate, w_up, [shard[:2] for shard in shards[early:]], ways, (pre,))
    early = len(shards)
    shards += [(ring(ahead, 1), ways // 2, 0), (ring(behind, -1), ways // 2, middle)]
    d_both, send, keep, merged = gradients(
        where, pre, shards, early, w_gate, w_up, d_hidden, error_fb, n_chips, ways
    )
    act = act_terms(d_both, w_gate, w_up)
    got = lax.ppermute(send, "core", SWAP)
    pieces = pair_sum(keep, got)
    pieces, act = lax.optimization_barrier((pieces, act))
    d_tokens = lax.psum_scatter(act, "tensor", scatter_dimension=1, tiled=True)
    pieces = lax.all_to_all(pieces, CHIPS, 0, 0, tiled=True)
    copies = mean_copies(pieces, n_chips * lax.axis_size("core"))
    own_half = lax.all_to_all(copies, CHIPS, 0, 0, tiled=True)
    other_half = lax.ppermute(own_half, "core", SWAP)
    new_error, q_next = finish(where, own_half, other_half, q_prev, merged)
    return (d_tokens, new_error.reshape(error_fb.shape), q_next.transpose(0, 2, 1))


def solution(mesh):
    chips_apart = Mesh(mesh.devices.reshape(4, 8, 2, 8), ("x", "z", "core", "tensor"))
    dp = ("x", "z", "core")
    return jax.shard_map(
        on_device,
        mesh=chips_apart,
        in_specs=(
            P(dp, "tensor"),
            P("tensor", None),
            P("tensor", None),
            P(dp, "tensor"),
            P(dp, None, "tensor", None),
            P(None, "tensor", None),
        ),
        out_specs=(P(dp, "tensor"), P(dp, None, "tensor", None), P(None, "tensor", None)),
        check_vma=False,
    )
```

```python
import functools
import math

import jax
import jax.numpy as jnp
from jax import lax
from jax.experimental import pallas as pl
from jax.experimental.pallas import tpu as pltpu
from jax.sharding import Mesh, PartitionSpec as P

HIGH_PRECISION = lax.Precision.HIGHEST
CHIPS = ("x", "z")
SWAP = ((0, 1), (1, 0))
VMEM_BYTES = 24 * 1024 * 1024


def three_parts(value):
    high = value.astype(jnp.bfloat16)
    rest = value - high.astype(jnp.float32)
    middle = rest.astype(jnp.bfloat16)
    low = (rest - middle.astype(jnp.float32)).astype(jnp.bfloat16)
    return high, middle, low


def inverse_cholesky(gram):
    n = gram.shape[0]
    row_ids = lax.broadcasted_iota(jnp.int32, (n, n), 0)
    col_ids = lax.broadcasted_iota(jnp.int32, (n, n), 1)
    work = jnp.concatenate([gram, jnp.where(row_ids == col_ids, 1.0, 0.0)], 1)
    blocks = [work[8 * k : 8 * k + 8] for k in range(n // 8)]
    below = lax.broadcasted_iota(jnp.int32, (8, 2 * n), 0)
    pivot = jnp.broadcast_to(blocks[0][0:1, 0:1], (1, 2 * n))
    for j in range(n - 1):
        k, i = divmod(j, 8)
        inverse = 1.0 / pivot
        scaled = blocks[k][i : i + 1] * inverse
        after, at = divmod(j + 1, 8)
        following = blocks[after][at : at + 1]
        beside = jnp.broadcast_to(following[:, j : j + 1], (1, 2 * n))
        pivot = jnp.broadcast_to(following[:, j + 1 : j + 2], (1, 2 * n)) - beside * beside * inverse
        for m in range(k, n // 8):
            if m == k and i == 7:
                continue
            factor = jnp.broadcast_to(blocks[m][:, j : j + 1], (8, 2 * n))
            if m == k:
                factor = jnp.where(below > i, factor, 0.0)
            blocks[m] = blocks[m] - factor * scaled
    work = jnp.concatenate(blocks, 0)
    pivots = jnp.sum(jnp.where(row_ids == col_ids, work[:, :n], 0.0), 1, keepdims=True)
    return work[:, n:] * lax.rsqrt(pivots)


def finish_kernel(where_ref, own_ref, other_ref, q_ref, merged_hbm, new_hbm, q_next_ref, stack_ref, merged_ref, new_ref, sem, out_sems):
    load = pltpu.make_async_copy(merged_hbm, merged_ref, sem)
    load.start()
    chunks, rows, lanes = own_ref.shape
    units, rank = 2 * rows, q_ref.shape[0]
    first = where_ref[0] == 0
    for j in range(chunks):
        at = slice(j * lanes, (j + 1) * lanes)
        stack_ref[0:rows, at] = jnp.where(first, own_ref[j], other_ref[j])
        stack_ref[rows:units, at] = jnp.where(first, other_ref[j], own_ref[j])
    q_parts = jnp.concatenate(three_parts(q_ref[...]), 0)
    width = chunks * lanes
    step = 1024
    for f in range(0, width, step):
        p_parts = jnp.dot(q_parts, stack_ref[0:units, f : f + step], preferred_element_type=jnp.float32)
        p_mean = p_parts[0:rank] + p_parts[rank : 2 * rank] + p_parts[2 * rank :]
        for k, part in enumerate(three_parts(p_mean)):
            stack_ref[units + k * rank : units + (k + 1) * rank, f : f + step] = part
    products = lax.dot_general(
        stack_ref[...], stack_ref[units:, :], (((1,), (1,)), ((), ())), preferred_element_type=jnp.float32
    )
    products = products[:, 0:rank] + products[:, rank : 2 * rank] + products[:, 2 * rank :]
    gram = products[units : units + rank] + products[units + rank : units + 2 * rank] + products[units + 2 * rank :]
    inverse = inverse_cholesky(gram)
    for k in range(2):
        q_next_ref[k] = lax.dot_general(
            inverse, products[k * rows : (k + 1) * rows], (((1,), (1,)), ((), ())),
            precision=HIGH_PRECISION, preferred_element_type=jnp.float32,
        )
    gram_inverse = jnp.dot(inverse.T, inverse, precision=HIGH_PRECISION, preferred_element_type=jnp.float32)
    weights = jnp.dot(
        products[0:units], gram_inverse, precision=HIGH_PRECISION, preferred_element_type=jnp.float32
    )
    high, middle, _ = three_parts(weights)
    factors = jnp.concatenate([high, high, middle], 1)
    load.wait()
    out = []
    for f in range(0, width, step):
        p_high = stack_ref[units : units + rank, f : f + step]
        p_middle = stack_ref[units + rank : units + 2 * rank, f : f + step]
        basis = jnp.concatenate([p_high, p_middle, p_high], 0)
        approximation = jnp.dot(factors, basis, preferred_element_type=jnp.float32)
        fresh = (merged_ref[:, f : f + step] - approximation).astype(jnp.bfloat16)
        new_ref[0, :, f : f + step] = fresh[0:rows]
        new_ref[1, :, f : f + step] = fresh[rows:]
        at = (slice(None), slice(None), pl.ds(f, step))
        copy = pltpu.make_async_copy(new_ref.at[at], new_hbm.at[at], out_sems.at[f // step])
        copy.start()
        out.append(copy)
    for copy in out:
        copy.wait()


def finish(where, own, other, q_prev, merged):
    rows = own.shape[1]
    width = own.shape[0] * own.shape[2]
    rank = q_prev.shape[2]
    vmem = pl.BlockSpec(memory_space=pltpu.VMEM)
    return pl.pallas_call(
        finish_kernel,
        out_shape=(
            jax.ShapeDtypeStruct((2, rows, width), jnp.bfloat16),
            jax.ShapeDtypeStruct((2, rank, rows), jnp.float32),
        ),
        in_specs=[pl.BlockSpec(memory_space=pltpu.SMEM), vmem, vmem, vmem, pl.BlockSpec(memory_space=pl.ANY)],
        out_specs=(pl.BlockSpec(memory_space=pl.ANY), vmem),
        scratch_shapes=[
            pltpu.VMEM((2 * rows + 3 * rank, width), jnp.bfloat16),
            pltpu.VMEM((2 * rows, width), jnp.float32),
            pltpu.VMEM((2, rows, width), jnp.bfloat16),
            pltpu.SemaphoreType.DMA,
            pltpu.SemaphoreType.DMA((width // 1024,)),
        ],
        compiler_params=pltpu.CompilerParams(vmem_limit_bytes=VMEM_BYTES),
        name="finish",
    )(where, own, other, q_prev.transpose(2, 0, 1).reshape(rank, 2 * rows), pltpu.with_memory_space_constraint(merged, pltpu.HBM))


def shard_offset(tensor_index, shift, start, shard_width, tensor_ways):
    shard = (tensor_index + shift + tensor_ways) % tensor_ways
    return pl.multiple_of(shard * shard_width + start, 128)


def add_products(pre, where_ref, gate_ref, up_ref, shards, shard_width, tensor_ways):
    for ref, shift, start in shards:
        at = pl.ds(shard_offset(where_ref[1], shift, start, shard_width, tensor_ways), ref.shape[1])
        weights = jnp.concatenate([gate_ref[:, at], up_ref[:, at]], 0)
        pre += lax.dot_general(weights, ref[...], (((1,), (1,)), ((), ())), preferred_element_type=jnp.float32)
    return pre


def early_kernel(where_ref, gate_ref, up_ref, *refs, shifts, shard_width, tensor_ways):
    shards = [(ref, shift, 0) for ref, shift in zip(refs, shifts)]
    before, pre_ref = refs[len(shifts) : -1], refs[-1]
    start = before[0][...] if before else jnp.zeros(pre_ref.shape, jnp.float32)
    pre_ref[...] = add_products(start, where_ref, gate_ref, up_ref, shards, shard_width, tensor_ways)


def early_products(where, w_gate, w_up, shards, tensor_ways, before=()):
    vmem = pl.BlockSpec(memory_space=pltpu.VMEM)
    return pl.pallas_call(
        functools.partial(
            early_kernel,
            shifts=[shift for _, shift in shards],
            shard_width=w_gate.shape[1] // tensor_ways,
            tensor_ways=tensor_ways,
        ),
        out_shape=jax.ShapeDtypeStruct((2 * w_gate.shape[0], shards[0][0].shape[0]), jnp.float32),
        in_specs=[pl.BlockSpec(memory_space=pltpu.SMEM)] + [vmem] * (2 + len(shards) + len(before)),
        out_specs=vmem,
        compiler_params=pltpu.CompilerParams(vmem_limit_bytes=VMEM_BYTES),
        name="early_products",
    )(where, w_gate, w_up, *[shard for shard, _ in shards], *before)


def gradient_kernel(where_ref, pre_ref, gate_ref, up_ref, cot_ref, error_ref, *refs, places, early, shard_width, tensor_ways, scale):
    sources = refs[: len(places)]
    d_ref, send_ref, keep_ref, merged_hbm, tokens_ref, send_buf, keep_buf, merged_ref, sems = refs[len(places) :]
    rows = gate_ref.shape[0]
    lanes = send_ref.shape[2]
    slots = []
    column = 0
    for source, (shift, start) in zip(sources, places):
        slots.append((tokens_ref.at[:, pl.ds(column, source.shape[1])], shift, start, column))
        column += source.shape[1]
    order = list(range(early, len(places))) + list(range(early))
    copies = [pltpu.make_async_copy(sources[i], slots[i][0], sems.at[i]) for i in range(len(places))]
    for i in order:
        copies[i].start()
    pre = pre_ref[...]
    for i in order[: len(places) - early]:
        copies[i].wait()
        pre = add_products(pre, where_ref, gate_ref, up_ref, [slots[i][:3]], shard_width, tensor_ways)
    gate_pre, up_pre = pre[0:rows], pre[rows:]
    squash = jax.nn.sigmoid(gate_pre)
    upstream = cot_ref[...].astype(jnp.float32)
    d_gate = (upstream * up_pre * squash * (1.0 + gate_pre * (1.0 - squash))).astype(jnp.bfloat16)
    d_up = (upstream * gate_pre * squash).astype(jnp.bfloat16)
    d_both = jnp.concatenate([d_gate, d_up], 0)
    d_ref[...] = d_both
    first = where_ref[0] == 0
    out = []
    for i in order:
        if i < early:
            copies[i].wait()
        ref, shift, start, column = slots[i]
        size = ref.shape[1]
        at = shard_offset(where_ref[1], shift, start, shard_width, tensor_ways)
        grads = jnp.dot(d_both, ref[...], preferred_element_type=jnp.float32) * scale
        gate_half = grads[0:rows] + error_ref[0, :, pl.ds(at, size)].astype(jnp.float32)
        up_half = grads[rows:] + error_ref[1, :, pl.ds(at, size)].astype(jnp.float32)
        merged_ref[0:rows, column : column + size] = gate_half
        merged_ref[rows:, column : column + size] = up_half
        gate_half = gate_half.astype(jnp.bfloat16)
        up_half = up_half.astype(jnp.bfloat16)
        keep = jnp.where(first, gate_half, up_half)
        send = jnp.where(first, up_half, gate_half)
        chunk, count = column // lanes, size // lanes
        for k in range(count):
            part = slice(k * lanes, (k + 1) * lanes)
            keep_buf[chunk + k] = keep[:, part]
            send_buf[chunk + k] = send[:, part]
        here, there = pl.ds(chunk, count), pl.ds(at // lanes, count)
        for source, target in (
            (send_buf.at[here], send_ref.at[there]),
            (keep_buf.at[here], keep_ref.at[there]),
            (merged_ref.at[:, pl.ds(column, size)], merged_hbm.at[:, pl.ds(at, size)]),
        ):
            copy = pltpu.make_async_copy(source, target, sems.at[len(places) + len(out)])
            copy.start()
            out.append(copy)
    for copy in out:
        copy.wait()


def gradients(where, pre, shards, early, w_gate, w_up, cot, error_fb, n_chips, tensor_ways):
    rows, width = w_gate.shape
    count = pre.shape[1]
    lanes = width // n_chips
    vmem = pl.BlockSpec(memory_space=pltpu.VMEM)
    here = pl.BlockSpec(memory_space=pl.ANY)
    last = 2
    operands = [pltpu.with_memory_space_constraint(shard, pltpu.HBM) for shard, _, _ in shards[:-last]]
    operands += [shard for shard, _, _ in shards[-last:]]
    return pl.pallas_call(
        functools.partial(
            gradient_kernel,
            places=[(shift, start) for _, shift, start in shards],
            early=early,
            shard_width=width // tensor_ways,
            tensor_ways=tensor_ways,
            scale=1.0 / math.sqrt(count),
        ),
        out_shape=(
            jax.ShapeDtypeStruct((2 * rows, count), jnp.bfloat16),
            pltpu.HBM((n_chips, rows, lanes), jnp.bfloat16),
            pltpu.HBM((n_chips, rows, lanes), jnp.bfloat16),
            pltpu.HBM((2 * rows, width), jnp.float32),
        ),
        in_specs=[pl.BlockSpec(memory_space=pltpu.SMEM)] + [vmem] * 5 + [here] * len(shards),
        out_specs=(vmem, here, here, here),
        scratch_shapes=[
            pltpu.VMEM((count, width), jnp.bfloat16),
            pltpu.VMEM((n_chips, rows, lanes), jnp.bfloat16),
            pltpu.VMEM((n_chips, rows, lanes), jnp.bfloat16),
            pltpu.VMEM((2 * rows, width), jnp.float32),
            pltpu.SemaphoreType.DMA((4 * len(shards),)),
        ],
        compiler_params=pltpu.CompilerParams(vmem_limit_bytes=VMEM_BYTES),
        name="gradients",
    )(where, pre, w_gate, w_up, cot.T, error_fb.reshape(2, rows, width), *operands)


def act_kernel(d_ref, gate_ref, up_ref, act_hbm, act_ref, sems):
    d_both = d_ref[...].T
    parts = sems.shape[0]
    step = act_ref.shape[1] // parts
    out = []
    for k in range(parts):
        at = slice(k * step, (k + 1) * step)
        weights = jnp.concatenate([gate_ref[:, at], up_ref[:, at]], 0)
        act_ref[:, at] = jnp.dot(d_both, weights, preferred_element_type=jnp.float32).astype(jnp.bfloat16)
        columns = (slice(None), pl.ds(k * step, step))
        out.append(pltpu.make_async_copy(act_ref.at[columns], act_hbm.at[columns], sems.at[k]))
        out[-1].start()
    for copy in out:
        copy.wait()


def act_terms(d_both, w_gate, w_up):
    vmem = pl.BlockSpec(memory_space=pltpu.VMEM)
    shape = (d_both.shape[1], w_gate.shape[1])
    return pl.pallas_call(
        act_kernel,
        out_shape=jax.ShapeDtypeStruct(shape, jnp.bfloat16),
        in_specs=[vmem] * 3,
        out_specs=pl.BlockSpec(memory_space=pl.ANY),
        scratch_shapes=[pltpu.VMEM(shape, jnp.bfloat16), pltpu.SemaphoreType.DMA((8,))],
        compiler_params=pltpu.CompilerParams(vmem_limit_bytes=VMEM_BYTES),
        name="act_terms",
    )(d_both, w_gate, w_up)


def pair_kernel(keep_hbm, got_ref, sum_ref, keep_ref, sems):
    parts = sems.shape[0]
    step = sum_ref.shape[0] // parts
    loads = []
    for k in range(parts):
        at = pl.ds(k * step, step)
        loads.append(pltpu.make_async_copy(keep_hbm.at[at], keep_ref.at[at], sems.at[k]))
        loads[-1].start()
    for k in range(parts):
        loads[k].wait()
        for i in range(k * step, (k + 1) * step):
            total = keep_ref[i].astype(jnp.float32) + got_ref[i].astype(jnp.float32)
            sum_ref[i] = total.astype(jnp.bfloat16)


def pair_sum(keep, got):
    vmem = pl.BlockSpec(memory_space=pltpu.VMEM)
    return pl.pallas_call(
        pair_kernel,
        out_shape=jax.ShapeDtypeStruct(keep.shape, jnp.bfloat16),
        in_specs=[pl.BlockSpec(memory_space=pl.ANY), vmem],
        out_specs=vmem,
        scratch_shapes=[pltpu.VMEM(keep.shape, jnp.bfloat16), pltpu.SemaphoreType.DMA((4,))],
        compiler_params=pltpu.CompilerParams(vmem_limit_bytes=VMEM_BYTES),
        name="pair_sum",
    )(pltpu.with_memory_space_constraint(keep, pltpu.HBM), got)


def mean_kernel(pieces_ref, copies_ref, *, scale):
    total = pieces_ref[0].astype(jnp.float32)
    for k in range(1, pieces_ref.shape[0]):
        total += pieces_ref[k].astype(jnp.float32)
    mean = (total * scale).astype(jnp.bfloat16)
    for k in range(copies_ref.shape[0]):
        copies_ref[k] = mean


def mean_copies(pieces, workers):
    vmem = pl.BlockSpec(memory_space=pltpu.VMEM)
    return pl.pallas_call(
        functools.partial(mean_kernel, scale=1.0 / workers),
        out_shape=jax.ShapeDtypeStruct(pieces.shape, jnp.bfloat16),
        in_specs=[vmem],
        out_specs=vmem,
        compiler_params=pltpu.CompilerParams(vmem_limit_bytes=VMEM_BYTES),
        name="mean_copies",
    )(pieces)


def ring(value, step):
    ways = lax.axis_size("tensor")
    return lax.ppermute(value, "tensor", [(i, (i + step) % ways) for i in range(ways)])


def on_device(tokens, w_gate, w_up, d_hidden, error_fb, q_prev):
    core = lax.axis_index("core")
    n_chips = lax.axis_size(CHIPS)
    ways = lax.axis_size("tensor")
    where = jnp.stack([core, lax.axis_index("tensor")])
    share = w_gate.shape[1] // ways

    shards = [(tokens, 0, 0)]
    ahead = behind = tokens
    for k in range(1, ways // 2):
        ahead, behind = ring(ahead, 1), ring(behind, -1)
        shards += [(ahead, -k, 0), (behind, k, 0)]
    early = 5
    pre = early_products(where, w_gate, w_up, [shard[:2] for shard in shards[:early]], ways)
    middle = share * 3 // 4
    ahead, behind, pre = lax.optimization_barrier((ahead[:, :middle], behind[:, middle:], pre))
    pre = early_products(where, w_gate, w_up, [shard[:2] for shard in shards[early:]], ways, (pre,))
    early = len(shards)
    shards += [(ring(ahead, 1), ways // 2, 0), (ring(behind, -1), ways // 2, middle)]
    d_both, send, keep, merged = gradients(
        where, pre, shards, early, w_gate, w_up, d_hidden, error_fb, n_chips, ways
    )
    act = act_terms(d_both, w_gate, w_up)
    got = lax.ppermute(send, "core", SWAP)
    pieces = pair_sum(keep, got)
    pieces, act = lax.optimization_barrier((pieces, act))
    d_tokens = lax.psum_scatter(act, "tensor", scatter_dimension=1, tiled=True)
    pieces = lax.all_to_all(pieces, CHIPS, 0, 0, tiled=True)
    copies = mean_copies(pieces, n_chips * lax.axis_size("core"))
    own_half = lax.all_to_all(copies, CHIPS, 0, 0, tiled=True)
    other_half = lax.ppermute(own_half, "core", SWAP)
    new_error, q_next = finish(where, own_half, other_half, q_prev, merged)
    return (d_tokens, new_error.reshape(error_fb.shape), q_next.transpose(0, 2, 1))


def solution(mesh):
    chips_apart = Mesh(mesh.devices.reshape(4, 8, 2, 8), ("x", "z", "core", "tensor"))
    dp = ("x", "z", "core")
    return jax.shard_map(
        on_device,
        mesh=chips_apart,
        in_specs=(
            P(dp, "tensor"),
            P("tensor", None),
            P("tensor", None),
            P(dp, "tensor"),
            P(dp, None, "tensor", None),
            P(None, "tensor", None),
        ),
        out_specs=(P(dp, "tensor"), P(dp, None, "tensor", None), P(None, "tensor", None)),
        check_vma=False,
    )
```

```python
import functools
import math

import jax
import jax.numpy as jnp
from jax import lax
from jax.experimental import pallas as pl
from jax.experimental.pallas import tpu as pltpu
from jax.sharding import Mesh, PartitionSpec as P

HIGH_PRECISION = lax.Precision.HIGHEST
CHIPS = ("x", "z")
SWAP = ((0, 1), (1, 0))
VMEM_BYTES = 24 * 1024 * 1024


def three_parts(value):
    high = value.astype(jnp.bfloat16)
    rest = value - high.astype(jnp.float32)
    middle = rest.astype(jnp.bfloat16)
    low = (rest - middle.astype(jnp.float32)).astype(jnp.bfloat16)
    return high, middle, low


def inverse_cholesky(gram):
    n = gram.shape[0]
    row_ids = lax.broadcasted_iota(jnp.int32, (n, n), 0)
    col_ids = lax.broadcasted_iota(jnp.int32, (n, n), 1)
    work = jnp.concatenate([gram, jnp.where(row_ids == col_ids, 1.0, 0.0)], 1)
    blocks = [work[8 * k : 8 * k + 8] for k in range(n // 8)]
    below = lax.broadcasted_iota(jnp.int32, (8, 2 * n), 0)
    pivot = jnp.broadcast_to(blocks[0][0:1, 0:1], (1, 2 * n))
    for j in range(n - 1):
        k, i = divmod(j, 8)
        inverse = 1.0 / pivot
        scaled = blocks[k][i : i + 1] * inverse
        after, at = divmod(j + 1, 8)
        following = blocks[after][at : at + 1]
        beside = jnp.broadcast_to(following[:, j : j + 1], (1, 2 * n))
        pivot = jnp.broadcast_to(following[:, j + 1 : j + 2], (1, 2 * n)) - beside * beside * inverse
        for m in range(k, n // 8):
            if m == k and i == 7:
                continue
            factor = jnp.broadcast_to(blocks[m][:, j : j + 1], (8, 2 * n))
            if m == k:
                factor = jnp.where(below > i, factor, 0.0)
            blocks[m] = blocks[m] - factor * scaled
    work = jnp.concatenate(blocks, 0)
    pivots = jnp.sum(jnp.where(row_ids == col_ids, work[:, :n], 0.0), 1, keepdims=True)
    return work[:, n:] * lax.rsqrt(pivots)


def finish_kernel(where_ref, own_ref, other_ref, q_ref, merged_hbm, new_hbm, q_next_ref, stack_ref, merged_ref, new_ref, sem, out_sems):
    load = pltpu.make_async_copy(merged_hbm, merged_ref, sem)
    load.start()
    chunks, rows, lanes = own_ref.shape
    units, rank = 2 * rows, q_ref.shape[0]
    first = where_ref[0] == 0
    for j in range(chunks):
        at = slice(j * lanes, (j + 1) * lanes)
        stack_ref[0:rows, at] = jnp.where(first, own_ref[j], other_ref[j])
        stack_ref[rows:units, at] = jnp.where(first, other_ref[j], own_ref[j])
    q_parts = jnp.concatenate(three_parts(q_ref[...]), 0)
    width = chunks * lanes
    step = 1024
    for f in range(0, width, step):
        p_parts = jnp.dot(q_parts, stack_ref[0:units, f : f + step], preferred_element_type=jnp.float32)
        p_mean = p_parts[0:rank] + p_parts[rank : 2 * rank] + p_parts[2 * rank :]
        for k, part in enumerate(three_parts(p_mean)):
            stack_ref[units + k * rank : units + (k + 1) * rank, f : f + step] = part
    products = lax.dot_general(
        stack_ref[...], stack_ref[units:, :], (((1,), (1,)), ((), ())), preferred_element_type=jnp.float32
    )
    products = products[:, 0:rank] + products[:, rank : 2 * rank] + products[:, 2 * rank :]
    gram = products[units : units + rank] + products[units + rank : units + 2 * rank] + products[units + 2 * rank :]
    inverse = inverse_cholesky(gram)
    for k in range(2):
        q_next_ref[k] = lax.dot_general(
            inverse, products[k * rows : (k + 1) * rows], (((1,), (1,)), ((), ())),
            precision=HIGH_PRECISION, preferred_element_type=jnp.float32,
        )
    gram_inverse = jnp.dot(inverse.T, inverse, precision=HIGH_PRECISION, preferred_element_type=jnp.float32)
    weights = jnp.dot(
        products[0:units], gram_inverse, precision=HIGH_PRECISION, preferred_element_type=jnp.float32
    )
    high, middle, _ = three_parts(weights)
    factors = jnp.concatenate([high, high, middle], 1)
    load.wait()
    out = []
    for f in range(0, width, step):
        p_high = stack_ref[units : units + rank, f : f + step]
        p_middle = stack_ref[units + rank : units + 2 * rank, f : f + step]
        basis = jnp.concatenate([p_high, p_middle, p_high], 0)
        approximation = jnp.dot(factors, basis, preferred_element_type=jnp.float32)
        fresh = (merged_ref[:, f : f + step] - approximation).astype(jnp.bfloat16)
        new_ref[0, :, f : f + step] = fresh[0:rows]
        new_ref[1, :, f : f + step] = fresh[rows:]
        at = (slice(None), slice(None), pl.ds(f, step))
        copy = pltpu.make_async_copy(new_ref.at[at], new_hbm.at[at], out_sems.at[f // step])
        copy.start()
        out.append(copy)
    for copy in out:
        copy.wait()


def finish(where, own, other, q_prev, merged):
    rows = own.shape[1]
    width = own.shape[0] * own.shape[2]
    rank = q_prev.shape[2]
    vmem = pl.BlockSpec(memory_space=pltpu.VMEM)
    return pl.pallas_call(
        finish_kernel,
        out_shape=(
            jax.ShapeDtypeStruct((2, rows, width), jnp.bfloat16),
            jax.ShapeDtypeStruct((2, rank, rows), jnp.float32),
        ),
        in_specs=[pl.BlockSpec(memory_space=pltpu.SMEM), vmem, vmem, vmem, pl.BlockSpec(memory_space=pl.ANY)],
        out_specs=(pl.BlockSpec(memory_space=pl.ANY), vmem),
        scratch_shapes=[
            pltpu.VMEM((2 * rows + 3 * rank, width), jnp.bfloat16),
            pltpu.VMEM((2 * rows, width), jnp.float32),
            pltpu.VMEM((2, rows, width), jnp.bfloat16),
            pltpu.SemaphoreType.DMA,
            pltpu.SemaphoreType.DMA((width // 1024,)),
        ],
        compiler_params=pltpu.CompilerParams(vmem_limit_bytes=VMEM_BYTES),
        name="finish",
    )(where, own, other, q_prev.transpose(2, 0, 1).reshape(rank, 2 * rows), pltpu.with_memory_space_constraint(merged, pltpu.HBM))


def shard_offset(tensor_index, shift, start, shard_width, tensor_ways):
    shard = (tensor_index + shift + tensor_ways) % tensor_ways
    return pl.multiple_of(shard * shard_width + start, 128)


def add_products(pre, where_ref, gate_ref, up_ref, shards, shard_width, tensor_ways):
    for ref, shift, start in shards:
        at = pl.ds(shard_offset(where_ref[1], shift, start, shard_width, tensor_ways), ref.shape[1])
        weights = jnp.concatenate([gate_ref[:, at], up_ref[:, at]], 0)
        pre += lax.dot_general(weights, ref[...], (((1,), (1,)), ((), ())), preferred_element_type=jnp.float32)
    return pre


def early_kernel(where_ref, gate_ref, up_ref, *refs, shifts, shard_width, tensor_ways):
    shards = [(ref, shift, 0) for ref, shift in zip(refs, shifts)]
    before, pre_ref = refs[len(shifts) : -1], refs[-1]
    start = before[0][...] if before else jnp.zeros(pre_ref.shape, jnp.float32)
    pre_ref[...] = add_products(start, where_ref, gate_ref, up_ref, shards, shard_width, tensor_ways)


def early_products(where, w_gate, w_up, shards, tensor_ways, before=()):
    vmem = pl.BlockSpec(memory_space=pltpu.VMEM)
    return pl.pallas_call(
        functools.partial(
            early_kernel,
            shifts=[shift for _, shift in shards],
            shard_width=w_gate.shape[1] // tensor_ways,
            tensor_ways=tensor_ways,
        ),
        out_shape=jax.ShapeDtypeStruct((2 * w_gate.shape[0], shards[0][0].shape[0]), jnp.float32),
        in_specs=[pl.BlockSpec(memory_space=pltpu.SMEM)] + [vmem] * (2 + len(shards) + len(before)),
        out_specs=vmem,
        compiler_params=pltpu.CompilerParams(vmem_limit_bytes=VMEM_BYTES),
        name="early_products",
    )(where, w_gate, w_up, *[shard for shard, _ in shards], *before)


def gradient_kernel(where_ref, pre_ref, gate_ref, up_ref, cot_ref, error_ref, *refs, places, early, shard_width, tensor_ways, scale):
    sources = refs[: len(places)]
    d_ref, send_ref, keep_ref, merged_hbm, tokens_ref, send_buf, keep_buf, merged_ref, sems = refs[len(places) :]
    rows = gate_ref.shape[0]
    lanes = send_ref.shape[2]
    slots = []
    column = 0
    for source, (shift, start) in zip(sources, places):
        slots.append((tokens_ref.at[:, pl.ds(column, source.shape[1])], shift, start, column))
        column += source.shape[1]
    order = list(range(early, len(places))) + list(range(early))
    copies = [pltpu.make_async_copy(sources[i], slots[i][0], sems.at[i]) for i in range(len(places))]
    for i in order:
        copies[i].start()
    pre = pre_ref[...]
    for i in order[: len(places) - early]:
        copies[i].wait()
        pre = add_products(pre, where_ref, gate_ref, up_ref, [slots[i][:3]], shard_width, tensor_ways)
    gate_pre, up_pre = pre[0:rows], pre[rows:]
    squash = jax.nn.sigmoid(gate_pre)
    upstream = cot_ref[...].astype(jnp.float32)
    d_gate = (upstream * up_pre * squash * (1.0 + gate_pre * (1.0 - squash))).astype(jnp.bfloat16)
    d_up = (upstream * gate_pre * squash).astype(jnp.bfloat16)
    d_both = jnp.concatenate([d_gate, d_up], 0)
    d_ref[...] = d_both
    first = where_ref[0] == 0
    out = []
    for i in order:
        if i < early:
            copies[i].wait()
        ref, shift, start, column = slots[i]
        size = ref.shape[1]
        at = shard_offset(where_ref[1], shift, start, shard_width, tensor_ways)
        grads = jnp.dot(d_both, ref[...], preferred_element_type=jnp.float32) * scale
        gate_half = grads[0:rows] + error_ref[0, :, pl.ds(at, size)].astype(jnp.float32)
        up_half = grads[rows:] + error_ref[1, :, pl.ds(at, size)].astype(jnp.float32)
        merged_ref[0:rows, column : column + size] = gate_half
        merged_ref[rows:, column : column + size] = up_half
        gate_half = gate_half.astype(jnp.bfloat16)
        up_half = up_half.astype(jnp.bfloat16)
        keep = jnp.where(first, gate_half, up_half)
        send = jnp.where(first, up_half, gate_half)
        chunk, count = column // lanes, size // lanes
        for k in range(count):
            part = slice(k * lanes, (k + 1) * lanes)
            keep_buf[chunk + k] = keep[:, part]
            send_buf[chunk + k] = send[:, part]
        here, there = pl.ds(chunk, count), pl.ds(at // lanes, count)
        for source, target in (
            (send_buf.at[here], send_ref.at[there]),
            (keep_buf.at[here], keep_ref.at[there]),
            (merged_ref.at[:, pl.ds(column, size)], merged_hbm.at[:, pl.ds(at, size)]),
        ):
            copy = pltpu.make_async_copy(source, target, sems.at[len(places) + len(out)])
            copy.start()
            out.append(copy)
    for copy in out:
        copy.wait()


def gradients(where, pre, shards, early, w_gate, w_up, cot, error_fb, n_chips, tensor_ways):
    rows, width = w_gate.shape
    count = pre.shape[1]
    lanes = width // n_chips
    vmem = pl.BlockSpec(memory_space=pltpu.VMEM)
    here = pl.BlockSpec(memory_space=pl.ANY)
    last = 2
    operands = [pltpu.with_memory_space_constraint(shard, pltpu.HBM) for shard, _, _ in shards[:-last]]
    operands += [shard for shard, _, _ in shards[-last:]]
    return pl.pallas_call(
        functools.partial(
            gradient_kernel,
            places=[(shift, start) for _, shift, start in shards],
            early=early,
            shard_width=width // tensor_ways,
            tensor_ways=tensor_ways,
            scale=1.0 / math.sqrt(count),
        ),
        out_shape=(
            jax.ShapeDtypeStruct((2 * rows, count), jnp.bfloat16),
            pltpu.HBM((n_chips, rows, lanes), jnp.bfloat16),
            pltpu.HBM((n_chips, rows, lanes), jnp.bfloat16),
            pltpu.HBM((2 * rows, width), jnp.float32),
        ),
        in_specs=[pl.BlockSpec(memory_space=pltpu.SMEM)] + [vmem] * 5 + [here] * len(shards),
        out_specs=(vmem, here, here, here),
        scratch_shapes=[
            pltpu.VMEM((count, width), jnp.bfloat16),
            pltpu.VMEM((n_chips, rows, lanes), jnp.bfloat16),
            pltpu.VMEM((n_chips, rows, lanes), jnp.bfloat16),
            pltpu.VMEM((2 * rows, width), jnp.float32),
            pltpu.SemaphoreType.DMA((4 * len(shards),)),
        ],
        compiler_params=pltpu.CompilerParams(vmem_limit_bytes=VMEM_BYTES),
        name="gradients",
    )(where, pre, w_gate, w_up, cot.T, error_fb.reshape(2, rows, width), *operands)


def act_kernel(d_ref, gate_ref, up_ref, act_hbm, act_ref, sems):
    d_both = d_ref[...].T
    parts = sems.shape[0]
    step = act_ref.shape[1] // parts
    out = []
    for k in range(parts):
        at = slice(k * step, (k + 1) * step)
        weights = jnp.concatenate([gate_ref[:, at], up_ref[:, at]], 0)
        act_ref[:, at] = jnp.dot(d_both, weights, preferred_element_type=jnp.float32).astype(jnp.bfloat16)
        columns = (slice(None), pl.ds(k * step, step))
        out.append(pltpu.make_async_copy(act_ref.at[columns], act_hbm.at[columns], sems.at[k]))
        out[-1].start()
    for copy in out:
        copy.wait()


def act_terms(d_both, w_gate, w_up):
    vmem = pl.BlockSpec(memory_space=pltpu.VMEM)
    shape = (d_both.shape[1], w_gate.shape[1])
    return pl.pallas_call(
        act_kernel,
        out_shape=jax.ShapeDtypeStruct(shape, jnp.bfloat16),
        in_specs=[vmem] * 3,
        out_specs=pl.BlockSpec(memory_space=pl.ANY),
        scratch_shapes=[pltpu.VMEM(shape, jnp.bfloat16), pltpu.SemaphoreType.DMA((8,))],
        compiler_params=pltpu.CompilerParams(vmem_limit_bytes=VMEM_BYTES),
        name="act_terms",
    )(d_both, w_gate, w_up)


def pair_kernel(keep_hbm, got_ref, sum_ref, keep_ref, sems):
    parts = sems.shape[0]
    step = sum_ref.shape[0] // parts
    loads = []
    for k in range(parts):
        at = pl.ds(k * step, step)
        loads.append(pltpu.make_async_copy(keep_hbm.at[at], keep_ref.at[at], sems.at[k]))
        loads[-1].start()
    for k in range(parts):
        loads[k].wait()
        for i in range(k * step, (k + 1) * step):
            total = keep_ref[i].astype(jnp.float32) + got_ref[i].astype(jnp.float32)
            sum_ref[i] = total.astype(jnp.bfloat16)


def pair_sum(keep, got):
    vmem = pl.BlockSpec(memory_space=pltpu.VMEM)
    return pl.pallas_call(
        pair_kernel,
        out_shape=jax.ShapeDtypeStruct(keep.shape, jnp.bfloat16),
        in_specs=[pl.BlockSpec(memory_space=pl.ANY), vmem],
        out_specs=vmem,
        scratch_shapes=[pltpu.VMEM(keep.shape, jnp.bfloat16), pltpu.SemaphoreType.DMA((4,))],
        compiler_params=pltpu.CompilerParams(vmem_limit_bytes=VMEM_BYTES),
        name="pair_sum",
    )(pltpu.with_memory_space_constraint(keep, pltpu.HBM), got)


def mean_kernel(pieces_ref, copies_ref, *, scale):
    total = pieces_ref[0].astype(jnp.float32)
    for k in range(1, pieces_ref.shape[0]):
        total += pieces_ref[k].astype(jnp.float32)
    mean = (total * scale).astype(jnp.bfloat16)
    for k in range(copies_ref.shape[0]):
        copies_ref[k] = mean


def mean_copies(pieces, workers):
    vmem = pl.BlockSpec(memory_space=pltpu.VMEM)
    return pl.pallas_call(
        functools.partial(mean_kernel, scale=1.0 / workers),
        out_shape=jax.ShapeDtypeStruct(pieces.shape, jnp.bfloat16),
        in_specs=[vmem],
        out_specs=vmem,
        compiler_params=pltpu.CompilerParams(vmem_limit_bytes=VMEM_BYTES),
        name="mean_copies",
    )(pieces)


def ring(value, step):
    ways = lax.axis_size("tensor")
    return lax.ppermute(value, "tensor", [(i, (i + step) % ways) for i in range(ways)])


def on_device(tokens, w_gate, w_up, d_hidden, error_fb, q_prev):
    core = lax.axis_index("core")
    n_chips = lax.axis_size(CHIPS)
    ways = lax.axis_size("tensor")
    where = jnp.stack([core, lax.axis_index("tensor")])
    share = w_gate.shape[1] // ways

    shards = [(tokens, 0, 0)]
    ahead = behind = tokens
    for k in range(1, ways // 2):
        ahead, behind = ring(ahead, 1), ring(behind, -1)
        shards += [(ahead, -k, 0), (behind, k, 0)]
    early = 5
    pre = early_products(where, w_gate, w_up, [shard[:2] for shard in shards[:early]], ways)
    middle = share * 3 // 4
    ahead, pre = lax.optimization_barrier((ahead[:, :middle], pre))
    behind = behind[:, middle:]
    pre = early_products(where, w_gate, w_up, [shard[:2] for shard in shards[early:]], ways, (pre,))
    early = len(shards)
    shards += [(ring(ahead, 1), ways // 2, 0), (ring(behind, -1), ways // 2, middle)]
    d_both, send, keep, merged = gradients(
        where, pre, shards, early, w_gate, w_up, d_hidden, error_fb, n_chips, ways
    )
    act = act_terms(d_both, w_gate, w_up)
    got = lax.ppermute(send, "core", SWAP)
    pieces = pair_sum(keep, got)
    pieces, act = lax.optimization_barrier((pieces, act))
    d_tokens = lax.psum_scatter(act, "tensor", scatter_dimension=1, tiled=True)
    pieces = lax.all_to_all(pieces, CHIPS, 0, 0, tiled=True)
    copies = mean_copies(pieces, n_chips * lax.axis_size("core"))
    own_half = lax.all_to_all(copies, CHIPS, 0, 0, tiled=True)
    other_half = lax.ppermute(own_half, "core", SWAP)
    new_error, q_next = finish(where, own_half, other_half, q_prev, merged)
    return (d_tokens, new_error.reshape(error_fb.shape), q_next.transpose(0, 2, 1))


def solution(mesh):
    chips_apart = Mesh(mesh.devices.reshape(4, 8, 2, 8), ("x", "z", "core", "tensor"))
    dp = ("x", "z", "core")
    return jax.shard_map(
        on_device,
        mesh=chips_apart,
        in_specs=(
            P(dp, "tensor"),
            P("tensor", None),
            P("tensor", None),
            P(dp, "tensor"),
            P(dp, None, "tensor", None),
            P(None, "tensor", None),
        ),
        out_specs=(P(dp, "tensor"), P(dp, None, "tensor", None), P(None, "tensor", None)),
        check_vma=False,
    )
```

```python
import functools
import math

import jax
import jax.numpy as jnp
from jax import lax
from jax.experimental import pallas as pl
from jax.experimental.pallas import tpu as pltpu
from jax.sharding import Mesh, PartitionSpec as P

HIGH_PRECISION = lax.Precision.HIGHEST
CHIPS = ("x", "z")
SWAP = ((0, 1), (1, 0))
VMEM_BYTES = 24 * 1024 * 1024


def three_parts(value):
    high = value.astype(jnp.bfloat16)
    rest = value - high.astype(jnp.float32)
    middle = rest.astype(jnp.bfloat16)
    low = (rest - middle.astype(jnp.float32)).astype(jnp.bfloat16)
    return high, middle, low


def inverse_cholesky(gram):
    n = gram.shape[0]
    row_ids = lax.broadcasted_iota(jnp.int32, (n, n), 0)
    col_ids = lax.broadcasted_iota(jnp.int32, (n, n), 1)
    work = jnp.concatenate([gram, jnp.where(row_ids == col_ids, 1.0, 0.0)], 1)
    blocks = [work[8 * k : 8 * k + 8] for k in range(n // 8)]
    below = lax.broadcasted_iota(jnp.int32, (8, 2 * n), 0)
    pivot = jnp.broadcast_to(blocks[0][0:1, 0:1], (1, 2 * n))
    for j in range(n - 1):
        k, i = divmod(j, 8)
        inverse = 1.0 / pivot
        scaled = blocks[k][i : i + 1] * inverse
        after, at = divmod(j + 1, 8)
        following = blocks[after][at : at + 1]
        beside = jnp.broadcast_to(following[:, j : j + 1], (1, 2 * n))
        pivot = jnp.broadcast_to(following[:, j + 1 : j + 2], (1, 2 * n)) - beside * beside * inverse
        for m in range(k, n // 8):
            if m == k and i == 7:
                continue
            factor = jnp.broadcast_to(blocks[m][:, j : j + 1], (8, 2 * n))
            if m == k:
                factor = jnp.where(below > i, factor, 0.0)
            blocks[m] = blocks[m] - factor * scaled
    work = jnp.concatenate(blocks, 0)
    pivots = jnp.sum(jnp.where(row_ids == col_ids, work[:, :n], 0.0), 1, keepdims=True)
    return work[:, n:] * lax.rsqrt(pivots)


def finish_kernel(where_ref, own_ref, other_ref, q_ref, merged_hbm, new_hbm, q_next_ref, stack_ref, merged_ref, new_ref, sem, out_sems):
    load = pltpu.make_async_copy(merged_hbm, merged_ref, sem)
    load.start()
    chunks, rows, lanes = own_ref.shape
    units, rank = 2 * rows, q_ref.shape[0]
    first = where_ref[0] == 0
    for j in range(chunks):
        at = slice(j * lanes, (j + 1) * lanes)
        stack_ref[0:rows, at] = jnp.where(first, own_ref[j], other_ref[j])
        stack_ref[rows:units, at] = jnp.where(first, other_ref[j], own_ref[j])
    q_parts = jnp.concatenate(three_parts(q_ref[...]), 0)
    width = chunks * lanes
    step = 1024
    for f in range(0, width, step):
        p_parts = jnp.dot(q_parts, stack_ref[0:units, f : f + step], preferred_element_type=jnp.float32)
        p_mean = p_parts[0:rank] + p_parts[rank : 2 * rank] + p_parts[2 * rank :]
        for k, part in enumerate(three_parts(p_mean)):
            stack_ref[units + k * rank : units + (k + 1) * rank, f : f + step] = part
    products = lax.dot_general(
        stack_ref[0 : units + 2 * rank, :],
        stack_ref[units:, :],
        (((1,), (1,)), ((), ())),
        preferred_element_type=jnp.float32,
    )
    lowest = products[units:, 2 * rank :]
    products = products[:, 0:rank] + products[:, rank : 2 * rank] + products[:, 2 * rank :]
    lowest = lowest[0:rank] + lowest[rank:]
    gram = products[units : units + rank] + products[units + rank :] + lowest.T
    inverse = inverse_cholesky(gram)
    for k in range(2):
        q_next_ref[k] = lax.dot_general(
            inverse, products[k * rows : (k + 1) * rows], (((1,), (1,)), ((), ())),
            precision=HIGH_PRECISION, preferred_element_type=jnp.float32,
        )
    gram_inverse = jnp.dot(inverse.T, inverse, precision=HIGH_PRECISION, preferred_element_type=jnp.float32)
    weights = jnp.dot(
        products[0:units], gram_inverse, precision=HIGH_PRECISION, preferred_element_type=jnp.float32
    )
    high, middle, _ = three_parts(weights)
    factors = jnp.concatenate([high, high, middle], 1)
    load.wait()
    out = []
    for f in range(0, width, step):
        p_high = stack_ref[units : units + rank, f : f + step]
        p_middle = stack_ref[units + rank : units + 2 * rank, f : f + step]
        basis = jnp.concatenate([p_high, p_middle, p_high], 0)
        approximation = jnp.dot(factors, basis, preferred_element_type=jnp.float32)
        fresh = (merged_ref[:, f : f + step] - approximation).astype(jnp.bfloat16)
        new_ref[0, :, f : f + step] = fresh[0:rows]
        new_ref[1, :, f : f + step] = fresh[rows:]
        at = (slice(None), slice(None), pl.ds(f, step))
        copy = pltpu.make_async_copy(new_ref.at[at], new_hbm.at[at], out_sems.at[f // step])
        copy.start()
        out.append(copy)
    for copy in out:
        copy.wait()


def finish(where, own, other, q_prev, merged):
    rows = own.shape[1]
    width = own.shape[0] * own.shape[2]
    rank = q_prev.shape[2]
    vmem = pl.BlockSpec(memory_space=pltpu.VMEM)
    return pl.pallas_call(
        finish_kernel,
        out_shape=(
            jax.ShapeDtypeStruct((2, rows, width), jnp.bfloat16),
            jax.ShapeDtypeStruct((2, rank, rows), jnp.float32),
        ),
        in_specs=[pl.BlockSpec(memory_space=pltpu.SMEM), vmem, vmem, vmem, pl.BlockSpec(memory_space=pl.ANY)],
        out_specs=(pl.BlockSpec(memory_space=pl.ANY), vmem),
        scratch_shapes=[
            pltpu.VMEM((2 * rows + 3 * rank, width), jnp.bfloat16),
            pltpu.VMEM((2 * rows, width), jnp.float32),
            pltpu.VMEM((2, rows, width), jnp.bfloat16),
            pltpu.SemaphoreType.DMA,
            pltpu.SemaphoreType.DMA((width // 1024,)),
        ],
        compiler_params=pltpu.CompilerParams(vmem_limit_bytes=VMEM_BYTES),
        name="finish",
    )(where, own, other, q_prev.transpose(2, 0, 1).reshape(rank, 2 * rows), pltpu.with_memory_space_constraint(merged, pltpu.HBM))


def shard_offset(tensor_index, shift, start, shard_width, tensor_ways):
    shard = (tensor_index + shift + tensor_ways) % tensor_ways
    return pl.multiple_of(shard * shard_width + start, 128)


def add_products(pre, where_ref, gate_ref, up_ref, shards, shard_width, tensor_ways):
    for ref, shift, start in shards:
        at = pl.ds(shard_offset(where_ref[1], shift, start, shard_width, tensor_ways), ref.shape[1])
        weights = jnp.concatenate([gate_ref[:, at], up_ref[:, at]], 0)
        pre += lax.dot_general(weights, ref[...], (((1,), (1,)), ((), ())), preferred_element_type=jnp.float32)
    return pre


def early_kernel(where_ref, gate_ref, up_ref, *refs, shifts, shard_width, tensor_ways):
    shards = [(ref, shift, 0) for ref, shift in zip(refs, shifts)]
    before, pre_ref = refs[len(shifts) : -1], refs[-1]
    start = before[0][...] if before else jnp.zeros(pre_ref.shape, jnp.float32)
    pre_ref[...] = add_products(start, where_ref, gate_ref, up_ref, shards, shard_width, tensor_ways)


def early_products(where, w_gate, w_up, shards, tensor_ways, before=()):
    vmem = pl.BlockSpec(memory_space=pltpu.VMEM)
    return pl.pallas_call(
        functools.partial(
            early_kernel,
            shifts=[shift for _, shift in shards],
            shard_width=w_gate.shape[1] // tensor_ways,
            tensor_ways=tensor_ways,
        ),
        out_shape=jax.ShapeDtypeStruct((2 * w_gate.shape[0], shards[0][0].shape[0]), jnp.float32),
        in_specs=[pl.BlockSpec(memory_space=pltpu.SMEM)] + [vmem] * (2 + len(shards) + len(before)),
        out_specs=vmem,
        compiler_params=pltpu.CompilerParams(vmem_limit_bytes=VMEM_BYTES),
        name="early_products",
    )(where, w_gate, w_up, *[shard for shard, _ in shards], *before)


def gradient_kernel(where_ref, pre_ref, gate_ref, up_ref, cot_ref, error_ref, *refs, places, early, shard_width, tensor_ways, scale):
    sources = refs[: len(places)]
    d_ref, send_ref, keep_ref, merged_hbm, tokens_ref, send_buf, keep_buf, merged_ref, sems = refs[len(places) :]
    rows = gate_ref.shape[0]
    lanes = send_ref.shape[2]
    slots = []
    column = 0
    for source, (shift, start) in zip(sources, places):
        slots.append((tokens_ref.at[:, pl.ds(column, source.shape[1])], shift, start, column))
        column += source.shape[1]
    order = list(range(early, len(places))) + list(range(early))
    copies = [pltpu.make_async_copy(sources[i], slots[i][0], sems.at[i]) for i in range(len(places))]
    for i in order:
        copies[i].start()
    pre = pre_ref[...]
    for i in order[: len(places) - early]:
        copies[i].wait()
        pre = add_products(pre, where_ref, gate_ref, up_ref, [slots[i][:3]], shard_width, tensor_ways)
    gate_pre, up_pre = pre[0:rows], pre[rows:]
    squash = jax.nn.sigmoid(gate_pre)
    upstream = cot_ref[...].astype(jnp.float32)
    d_gate = (upstream * up_pre * squash * (1.0 + gate_pre * (1.0 - squash))).astype(jnp.bfloat16)
    d_up = (upstream * gate_pre * squash).astype(jnp.bfloat16)
    d_both = jnp.concatenate([d_gate, d_up], 0)
    d_ref[...] = d_both
    first = where_ref[0] == 0
    out = []
    for i in order:
        if i < early:
            copies[i].wait()
        ref, shift, start, column = slots[i]
        size = ref.shape[1]
        at = shard_offset(where_ref[1], shift, start, shard_width, tensor_ways)
        grads = jnp.dot(d_both, ref[...], preferred_element_type=jnp.float32) * scale
        gate_half = grads[0:rows] + error_ref[0, :, pl.ds(at, size)].astype(jnp.float32)
        up_half = grads[rows:] + error_ref[1, :, pl.ds(at, size)].astype(jnp.float32)
        merged_ref[0:rows, column : column + size] = gate_half
        merged_ref[rows:, column : column + size] = up_half
        gate_half = gate_half.astype(jnp.bfloat16)
        up_half = up_half.astype(jnp.bfloat16)
        keep = jnp.where(first, gate_half, up_half)
        send = jnp.where(first, up_half, gate_half)
        chunk, count = column // lanes, size // lanes
        for k in range(count):
            part = slice(k * lanes, (k + 1) * lanes)
            keep_buf[chunk + k] = keep[:, part]
            send_buf[chunk + k] = send[:, part]
        here, there = pl.ds(chunk, count), pl.ds(at // lanes, count)
        for source, target in (
            (send_buf.at[here], send_ref.at[there]),
            (keep_buf.at[here], keep_ref.at[there]),
            (merged_ref.at[:, pl.ds(column, size)], merged_hbm.at[:, pl.ds(at, size)]),
        ):
            copy = pltpu.make_async_copy(source, target, sems.at[len(places) + len(out)])
            copy.start()
            out.append(copy)
    for copy in out:
        copy.wait()


def gradients(where, pre, shards, early, w_gate, w_up, cot, error_fb, n_chips, tensor_ways):
    rows, width = w_gate.shape
    count = pre.shape[1]
    lanes = width // n_chips
    vmem = pl.BlockSpec(memory_space=pltpu.VMEM)
    here = pl.BlockSpec(memory_space=pl.ANY)
    last = 2
    operands = [pltpu.with_memory_space_constraint(shard, pltpu.HBM) for shard, _, _ in shards[:-last]]
    operands += [shard for shard, _, _ in shards[-last:]]
    return pl.pallas_call(
        functools.partial(
            gradient_kernel,
            places=[(shift, start) for _, shift, start in shards],
            early=early,
            shard_width=width // tensor_ways,
            tensor_ways=tensor_ways,
            scale=1.0 / math.sqrt(count),
        ),
        out_shape=(
            jax.ShapeDtypeStruct((2 * rows, count), jnp.bfloat16),
            pltpu.HBM((n_chips, rows, lanes), jnp.bfloat16),
            pltpu.HBM((n_chips, rows, lanes), jnp.bfloat16),
            pltpu.HBM((2 * rows, width), jnp.float32),
        ),
        in_specs=[pl.BlockSpec(memory_space=pltpu.SMEM)] + [vmem] * 5 + [here] * len(shards),
        out_specs=(vmem, here, here, here),
        scratch_shapes=[
            pltpu.VMEM((count, width), jnp.bfloat16),
            pltpu.VMEM((n_chips, rows, lanes), jnp.bfloat16),
            pltpu.VMEM((n_chips, rows, lanes), jnp.bfloat16),
            pltpu.VMEM((2 * rows, width), jnp.float32),
            pltpu.SemaphoreType.DMA((4 * len(shards),)),
        ],
        compiler_params=pltpu.CompilerParams(vmem_limit_bytes=VMEM_BYTES),
        name="gradients",
    )(where, pre, w_gate, w_up, cot.T, error_fb.reshape(2, rows, width), *operands)


def act_kernel(d_ref, gate_ref, up_ref, act_hbm, act_ref, sems):
    d_both = d_ref[...].T
    parts = sems.shape[0]
    step = act_ref.shape[1] // parts
    out = []
    for k in range(parts):
        at = slice(k * step, (k + 1) * step)
        weights = jnp.concatenate([gate_ref[:, at], up_ref[:, at]], 0)
        act_ref[:, at] = jnp.dot(d_both, weights, preferred_element_type=jnp.float32).astype(jnp.bfloat16)
        columns = (slice(None), pl.ds(k * step, step))
        out.append(pltpu.make_async_copy(act_ref.at[columns], act_hbm.at[columns], sems.at[k]))
        out[-1].start()
    for copy in out:
        copy.wait()


def act_terms(d_both, w_gate, w_up):
    vmem = pl.BlockSpec(memory_space=pltpu.VMEM)
    shape = (d_both.shape[1], w_gate.shape[1])
    return pl.pallas_call(
        act_kernel,
        out_shape=jax.ShapeDtypeStruct(shape, jnp.bfloat16),
        in_specs=[vmem] * 3,
        out_specs=pl.BlockSpec(memory_space=pl.ANY),
        scratch_shapes=[pltpu.VMEM(shape, jnp.bfloat16), pltpu.SemaphoreType.DMA((8,))],
        compiler_params=pltpu.CompilerParams(vmem_limit_bytes=VMEM_BYTES),
        name="act_terms",
    )(d_both, w_gate, w_up)


def pair_kernel(keep_hbm, got_ref, sum_ref, keep_ref, sems):
    parts = sems.shape[0]
    step = sum_ref.shape[0] // parts
    loads = []
    for k in range(parts):
        at = pl.ds(k * step, step)
        loads.append(pltpu.make_async_copy(keep_hbm.at[at], keep_ref.at[at], sems.at[k]))
        loads[-1].start()
    for k in range(parts):
        loads[k].wait()
        for i in range(k * step, (k + 1) * step):
            total = keep_ref[i].astype(jnp.float32) + got_ref[i].astype(jnp.float32)
            sum_ref[i] = total.astype(jnp.bfloat16)


def pair_sum(keep, got):
    vmem = pl.BlockSpec(memory_space=pltpu.VMEM)
    return pl.pallas_call(
        pair_kernel,
        out_shape=jax.ShapeDtypeStruct(keep.shape, jnp.bfloat16),
        in_specs=[pl.BlockSpec(memory_space=pl.ANY), vmem],
        out_specs=vmem,
        scratch_shapes=[pltpu.VMEM(keep.shape, jnp.bfloat16), pltpu.SemaphoreType.DMA((4,))],
        compiler_params=pltpu.CompilerParams(vmem_limit_bytes=VMEM_BYTES),
        name="pair_sum",
    )(pltpu.with_memory_space_constraint(keep, pltpu.HBM), got)


def mean_kernel(pieces_ref, copies_ref, *, scale):
    total = pieces_ref[0].astype(jnp.float32)
    for k in range(1, pieces_ref.shape[0]):
        total += pieces_ref[k].astype(jnp.float32)
    mean = (total * scale).astype(jnp.bfloat16)
    for k in range(copies_ref.shape[0]):
        copies_ref[k] = mean


def mean_copies(pieces, workers):
    vmem = pl.BlockSpec(memory_space=pltpu.VMEM)
    return pl.pallas_call(
        functools.partial(mean_kernel, scale=1.0 / workers),
        out_shape=jax.ShapeDtypeStruct(pieces.shape, jnp.bfloat16),
        in_specs=[vmem],
        out_specs=vmem,
        compiler_params=pltpu.CompilerParams(vmem_limit_bytes=VMEM_BYTES),
        name="mean_copies",
    )(pieces)


def ring(value, step):
    ways = lax.axis_size("tensor")
    return lax.ppermute(value, "tensor", [(i, (i + step) % ways) for i in range(ways)])


def on_device(tokens, w_gate, w_up, d_hidden, error_fb, q_prev):
    core = lax.axis_index("core")
    n_chips = lax.axis_size(CHIPS)
    ways = lax.axis_size("tensor")
    where = jnp.stack([core, lax.axis_index("tensor")])
    share = w_gate.shape[1] // ways

    shards = [(tokens, 0, 0)]
    ahead = behind = tokens
    for k in range(1, ways // 2):
        ahead, behind = ring(ahead, 1), ring(behind, -1)
        shards += [(ahead, -k, 0), (behind, k, 0)]
    early = 5
    pre = early_products(where, w_gate, w_up, [shard[:2] for shard in shards[:early]], ways)
    middle = share * 3 // 4
    ahead, pre = lax.optimization_barrier((ahead[:, :middle], pre))
    behind = behind[:, middle:]
    pre = early_products(where, w_gate, w_up, [shard[:2] for shard in shards[early:]], ways, (pre,))
    early = len(shards)
    shards += [(ring(ahead, 1), ways // 2, 0), (ring(behind, -1), ways // 2, middle)]
    d_both, send, keep, merged = gradients(
        where, pre, shards, early, w_gate, w_up, d_hidden, error_fb, n_chips, ways
    )
    act = act_terms(d_both, w_gate, w_up)
    got = lax.ppermute(send, "core", SWAP)
    pieces = pair_sum(keep, got)
    pieces, act = lax.optimization_barrier((pieces, act))
    d_tokens = lax.psum_scatter(act, "tensor", scatter_dimension=1, tiled=True)
    pieces = lax.all_to_all(pieces, CHIPS, 0, 0, tiled=True)
    copies = mean_copies(pieces, n_chips * lax.axis_size("core"))
    own_half = lax.all_to_all(copies, CHIPS, 0, 0, tiled=True)
    other_half = lax.ppermute(own_half, "core", SWAP)
    new_error, q_next = finish(where, own_half, other_half, q_prev, merged)
    return (d_tokens, new_error.reshape(error_fb.shape), q_next.transpose(0, 2, 1))


def solution(mesh):
    chips_apart = Mesh(mesh.devices.reshape(4, 8, 2, 8), ("x", "z", "core", "tensor"))
    dp = ("x", "z", "core")
    return jax.shard_map(
        on_device,
        mesh=chips_apart,
        in_specs=(
            P(dp, "tensor"),
            P("tensor", None),
            P("tensor", None),
            P(dp, "tensor"),
            P(dp, None, "tensor", None),
            P(None, "tensor", None),
        ),
        out_specs=(P(dp, "tensor"), P(dp, None, "tensor", None), P(None, "tensor", None)),
        check_vma=False,
    )
```
